32 devices in a mesh: gx: 2 (over core), gy: 4 (over y, x), gz: 4 (over z).
Axes of the slice: x: 2, y: 2, z: 4, core: 2. Of those that a mesh axis runs over, the one named last changes fastest.
Arguments:
- adjoint_final: float32 [16, 32, 512], P('gz', 'gx', 'gy'), may hold values from -6 to 6
- conductivity: float32 [3, 16, 32, 512], P(None, 'gz', 'gx', 'gy'), may hold values from 0.05 to 1
- step_ratio: float32 [16, 32, 512], P('gz', 'gx', 'gy'), may hold values from 0.04 to 0.16
- refine_rate: float32 [16, 32, 512], P('gz', 'gx', 'gy'), may hold values from 0.05 to 0.24
- residual: float32 [4, 512], P(None, ('gx', 'gy')), may hold values from -6 to 6
- sensor_tile: int32 [512], P(('gx', 'gy')), may hold values from 0 to 7, as said below
- sensor_cell: int32 [512], P(('gx', 'gy')), may hold values from 0 to 32767
- substeps: int32 [2, 4], replicated, may hold values from 1 to 6, as said below
Outputs:
- adjoint_start: float32 [16, 32, 512], P('gz', 'gx', 'gy')
- sensitivity: float32 [16, 32, 512], P('gz', 'gx', 'gy')
The draws below stay inside these ranges and needn't reach their ends.
Inputs may be any that keep to these rules, and one draw needn't show every extreme that they name: `sensor_tile`: tiles are numbered ix * 4 + iy. Among the 64 sensors of each aligned block at most 10 name one tile, and in every block some tile is named by exactly 10 of them. `substeps`: some tile takes 6 sub-steps in every draw.
All inputs are finite; a program needn't handle non-finite values.
Results may differ from the reference program's by a relative error of at most 0.000079.
Values sent between devices are 32-bit elements; how exact they have to be, the bound alone decides.
A program may use at most 64 MiB of HBM per device.

```python
import math
import jax
import jax.numpy as jnp

CX = 16
CY = 128
NS_DEV = 64
STEPS = 4
MAXSUB = 6
TGX = 2
TGY = 4
TILES = 8
NX = 32
NY = 512
NZ = 16
SENSORS = 512
SLOTS = 10
N_GX = 2
N_GY = 4


def draw_sensor_tile(key, part):
    key_hot, key_other, key_order = jax.random.split(key, 3)
    hottest = jax.random.randint(key_hot, (), 0, TILES)
    others = jax.vmap(lambda sub: jax.random.permutation(sub, TILES - 1))(jax.random.split(key_other, TILES))
    places = jnp.arange(NS_DEV)
    picked = others[:, (places - SLOTS) % (TILES - 1)]
    picked = picked + (picked >= hottest).astype(jnp.int32)
    tiles = jnp.where(places[None, :] < SLOTS, hottest, picked)
    orders = jax.vmap(lambda sub: jax.random.permutation(sub, NS_DEV))(jax.random.split(key_order, TILES))
    tiles = jnp.take_along_axis(tiles, orders, axis=1)
    return tiles.reshape(-1).astype(jnp.int32)


def draw_substeps(key, part):
    key_base, key_hot, key_force = jax.random.split(key, 3)
    baseline = jax.random.randint(key_base, (TGX, TGY), 1, 3)
    heated = jax.random.randint(key_hot, (TGX, TGY), 0, 8) == 0
    forced = jax.random.randint(key_force, (), 0, TILES)
    heated = heated.reshape(-1) | (jnp.arange(TILES) == forced)
    return jnp.where(heated.reshape(TGX, TGY), MAXSUB, baseline).astype(jnp.int32)


def set_ends(values, key, low, top_value):
    dims = values.shape
    place = [jax.random.randint(jax.random.fold_in(key, axis), (), 0, dims[axis]) for axis in range(len(dims))]
    values = values.at[tuple(place)].set(low)
    longest = dims.index(max(dims))
    place[longest] = (place[longest] + 1) % dims[longest]
    return values.at[tuple(place)].set(top_value)


def levels(rng, dims, shards, low, largest):
    level = 1.0
    for axis_at, shards_of in shards:
        draws = jax.random.uniform(jax.random.fold_in(jax.random.fold_in(rng, 6), axis_at), (shards_of,), jnp.float32, low / len(shards), largest / len(shards))
        level = level * jnp.repeat(jnp.exp(draws), dims[axis_at] // shards_of).reshape((-1,) + (1,) * (len(dims) - 1 - axis_at))
    return level


def gaussian(key, dims, spread, reach, shards=(), dtype=jnp.bfloat16):
    result = jax.random.normal(key, dims, jnp.float32) * spread
    if len(shards) > 0:
        result = levels(key, dims, shards, -0.22, 0.18) * result
    return jnp.clip(result, min=-reach, max=reach).astype(dtype)


def setup_inputs(seed: int = 0) -> dict:
    seeds = jax.random.split(jax.random.key(seed), 9)
    return {
        "adjoint_final": gaussian(seeds[0], (NZ, NX, NY), 1.0, 6.0, ((0, 4), (1, 2), (2, 4)), jnp.float32),
        "conductivity": jnp.clip(jnp.exp(math.log(1.0) - 2.9957323 * jax.random.uniform(seeds[1], (3, NZ, NX, NY), jnp.float32) ** levels(seeds[1], (3, NZ, NX, NY), ((1, 4), (2, 2), (3, 4)), -0.2, 0.2)), 0.05, 1.0),
        "step_ratio": jnp.clip(jnp.exp(math.log(0.16) - 1.3862944 * jax.random.uniform(seeds[2], (NZ, NX, NY), jnp.float32) ** levels(seeds[2], (NZ, NX, NY), ((0, 4), (1, 2), (2, 4)), -0.2, 0.2)), 0.04, 0.16),
        "refine_rate": jnp.clip(jnp.exp(math.log(0.24) - 1.5686159 * jax.random.uniform(seeds[3], (NZ, NX, NY), jnp.float32) ** levels(seeds[3], (NZ, NX, NY), ((0, 4), (1, 2), (2, 4)), -0.2, 0.2)), 0.05, 0.24),
        "residual": gaussian(seeds[4], (STEPS, SENSORS), 1.0, 6.0, ((1, 8),), jnp.float32),
        "sensor_tile": draw_sensor_tile(jax.random.fold_in(seeds[8], 71), 0),
        "sensor_cell": set_ends(jax.random.randint(seeds[6], (SENSORS,), 0, NZ * CX * CY), jax.random.fold_in(seeds[6], 1), 0, (NZ * CX * CY) - 1).astype(jnp.int32),
        "substeps": draw_substeps(jax.random.fold_in(seeds[8], 71), 0),
    }


def harmonic(first, second):
    return 2.0 * first * second / (first + second)


def lateral_tiles(field):
    down_diff = field[:, :, 1:] - field[:, :, :-1]
    side_diff = field[..., 1:] - field[..., :-1]
    rows_part = jnp.pad(down_diff, ((0, 0), (0, 0), (0, 1), (0, 0), (0, 0))) - jnp.pad(down_diff, ((0, 0), (0, 0), (1, 0), (0, 0), (0, 0)))
    cols_part = jnp.pad(side_diff, ((0, 0), (0, 0), (0, 0), (0, 0), (0, 1))) - jnp.pad(side_diff, ((0, 0), (0, 0), (0, 0), (0, 0), (1, 0)))
    return rows_part + cols_part


def reference(adjoint_final, conductivity, step_ratio, refine_rate, residual, sensor_tile, sensor_cell, substeps):
    padded = jnp.pad(conductivity, ((0, 0), (1, 1), (1, 1), (1, 1)))
    row_up = harmonic(conductivity[0], padded[0, 1:-1, 2:, 1:-1])
    row_down = harmonic(conductivity[0], padded[0, 1:-1, :-2, 1:-1])
    col_up = harmonic(conductivity[1], padded[1, 1:-1, 1:-1, 2:])
    col_down = harmonic(conductivity[1], padded[1, 1:-1, 1:-1, :-2])
    layer_up = harmonic(conductivity[2], padded[2, 2:, 1:-1, 1:-1])
    layer_down = harmonic(conductivity[2], padded[2, :-2, 1:-1, 1:-1])
    tile_row = sensor_tile // N_GY
    tile_col = sensor_tile % N_GY
    layer_of = sensor_cell // (CX * CY)
    within = sensor_cell % (CX * CY)
    grid_row = tile_row * CX + within // CY
    grid_col = tile_col * CY + within % CY
    target = (layer_of * (NX * NY) + grid_row * NY + grid_col).astype(jnp.int32)
    counts = substeps[None, :, None, :, None]
    rates = refine_rate.reshape(NZ, N_GX, CX, N_GY, CY)
    adjoint = adjoint_final
    sensitivity = jnp.zeros_like(adjoint_final)
    for step_index in range(STEPS - 1, -1, -1):
        flat = adjoint.reshape(-1).at[target].add(residual[step_index])
        adjoint = flat.reshape(NZ, NX, NY)
        weighted = step_ratio * adjoint
        wpad = jnp.pad(weighted, 1)
        adjoint = adjoint + (row_up * (wpad[1:-1, 2:, 1:-1] - weighted) + row_down * (wpad[1:-1, :-2, 1:-1] - weighted)
                             + col_up * (wpad[1:-1, 1:-1, 2:] - weighted) + col_down * (wpad[1:-1, 1:-1, :-2] - weighted)
                             + layer_up * (wpad[2:, 1:-1, 1:-1] - weighted) + layer_down * (wpad[:-2, 1:-1, 1:-1] - weighted))
        tiled = adjoint.reshape(NZ, N_GX, CX, N_GY, CY)
        for turn in range(MAXSUB):
            tiled = jnp.where(counts > turn, tiled + lateral_tiles(rates * tiled), tiled)
        adjoint = tiled.reshape(NZ, NX, NY)
        sensitivity = sensitivity + step_ratio * adjoint
    return adjoint, sensitivity
```

```python
import functools

import jax
import jax.numpy as jnp
from jax import lax
from jax.experimental import pallas as pl
from jax.experimental.pallas import tpu as pltpu
from jax.sharding import PartitionSpec as P

MESH = pl.DeviceIdType.MESH
MOST_TURNS = 6
SUB = 8
NT = (((1,), (1,)), ((), ()))


def harmonic(first, second):
    return 2.0 * first * second / (first + second)


def pieces_of(values):
    high = values.astype(jnp.bfloat16).astype(jnp.float32)
    rest = values - high
    middle = rest.astype(jnp.bfloat16).astype(jnp.float32)
    return high, middle, rest - middle


def kernel(
    sizes,
    cond_hbm,
    adjoint_hbm,
    ratio_hbm,
    rate_hbm,
    res_hbm,
    tile_hbm,
    cell_hbm,
    substeps_ref,
    adjoint_out,
    sens_out,
    base,
    res_in,
    tile_in,
    cell_in,
    sensors,
    gathered,
    first_x,
    first_x_in,
    first_y,
    first_y_in,
    first_z_in,
    send_w,
    send_x,
    recv_x,
    send_y,
    recv_y,
    recv_z,
    load_sem,
    sensor_send,
    sensor_recv,
    halo_send,
    halo_recv,
):
    nx, ny, nz, layers, rows, cols, steps, listed = sizes
    cells = layers * rows
    groups_of_rows = cells // SUB
    tiles = nx * ny
    x, y, z = lax.axis_index("gx"), lax.axis_index("gy"), lax.axis_index("gz")
    me = x * ny + y

    loads = [
        pltpu.make_async_copy(src, dst, load_sem.at[k])
        for k, (src, dst) in enumerate(
            (
                (res_hbm, res_in),
                (tile_hbm, tile_in),
                (cell_hbm, cell_in),
                (adjoint_hbm, base.at[3]),
                (ratio_hbm, base.at[4]),
                (cond_hbm, base.at[pl.ds(0, 3)]),
                (rate_hbm, base.at[5]),
            )
        )
    ]
    for load in loads:
        load.start()

    for ref in (first_x_in, first_y_in, first_z_in, recv_x, recv_y, recv_z, sensors):
        ref[...] = jnp.zeros_like(ref)

    sides = (
        (0, nx, x, -1),
        (0, nx, x, 1),
        (1, ny, y, -1),
        (1, ny, y, 1),
        (2, nz, z, -1),
        (2, nz, z, 1),
    )

    def device_at(axis, step):
        place = [x, y, z]
        place[axis] = place[axis] + step
        return tuple(place)

    def inside(count, place, step):
        return place > 0 if step < 0 else place < count - 1

    barrier = pltpu.get_barrier_semaphore()

    def sensor_peer(offset):
        there = lax.rem(me + offset, tiles)
        return (lax.div(there, ny), lax.rem(there, ny), z)

    for offset in range(1, tiles):
        pl.semaphore_signal(barrier, inc=1, device_id=sensor_peer(offset), device_id_type=MESH)
    for axis, count, place, step in sides[4:]:

        @pl.when(inside(count, place, step))
        def _():
            pl.semaphore_signal(
                barrier, inc=1, device_id=device_at(axis, step), device_id_type=MESH
            )

    for load in loads[:3]:
        load.wait()
    per = max(1, cols // listed)
    lane = lax.broadcasted_iota(jnp.int32, (1, cols), 1)
    cell = cell_in[...]
    grid_layers_rows = nz * cells
    key = tile_in[...] * grid_layers_rows + lax.div(cell, cols)
    column = lax.rem(cell, cols)
    for slot in range(per):
        here = pl.ds(slot * listed, listed)
        sensors[0:steps, here] = res_in[...]
        sensors[steps : steps + 1, here] = key.astype(jnp.float32)
        sensors[steps + 1 : steps + 2, here] = column.astype(jnp.float32)
    if per > 1:
        mine = lax.div(lane, listed) == lax.rem(me, per)
        sensors[...] = jnp.where(mine, sensors[...], 0.0)
    gathered[me] = sensors[...]

    for load in loads[3:]:
        load.wait()
    lanes = lax.broadcasted_iota(jnp.int32, (SUB, cols), 1)

    def pack_columns(arrays):
        to_left = jnp.zeros((SUB, cols), jnp.float32)
        to_right = jnp.zeros((SUB, cols), jnp.float32)
        spot = 0
        for array in arrays:
            for part in range(groups_of_rows):
                block = array[part * SUB : (part + 1) * SUB, :]
                left = pltpu.roll(block, spot % cols, 1)
                right = pltpu.roll(block, (spot + 2) % cols, 1)
                to_left = jnp.where(lanes == spot, left, to_left)
                to_right = jnp.where(lanes == spot + 1, right, to_right)
                spot += 2
        return to_left, to_right

    def unpack_columns(packed, spot):
        return jnp.concatenate(
            [
                pltpu.roll(packed, (cols - 2 * (spot + part) - 1) % cols, 1)
                for part in range(groups_of_rows)
            ],
            axis=0,
        )

    def pick_rows(array, row):
        return jnp.concatenate(
            [array[level * rows + row : level * rows + row + 1, :] for level in range(layers)],
            axis=0,
        )

    def spread_rows(low, high):
        half = rows // 2
        parts = []
        for level in range(layers):
            parts.append(jnp.broadcast_to(low[level : level + 1, :], (half, cols)))
            parts.append(jnp.broadcast_to(high[level : level + 1, :], (rows - half, cols)))
        return jnp.concatenate(parts, axis=0)

    c0, c1, c2 = base[0], base[1], base[2]
    adjoint, ratio, rate = base[3], base[4], base[5]

    for k, array in enumerate((adjoint, ratio, c0)):
        first_x[0, k * layers : (k + 1) * layers, :] = pick_rows(array, 0)
        first_x[1, k * layers : (k + 1) * layers, :] = pick_rows(array, rows - 1)
    left, right = pack_columns((adjoint, ratio, c1))
    first_y[0] = left
    first_y[1] = right

    neighbours = (
        (tiles - 1)
        + (z > 0).astype(jnp.int32)
        + (z < nz - 1).astype(jnp.int32)
    )
    pl.semaphore_wait(barrier, neighbours)

    def sensor_copy(offset):
        return pltpu.make_async_remote_copy(
            src_ref=sensors,
            dst_ref=gathered.at[me],
            send_sem=sensor_send.at[offset],
            recv_sem=sensor_recv.at[offset],
            device_id=sensor_peer(offset),
            device_id_type=MESH,
        )

    def sensor_arrival(offset):
        origin = lax.rem(me + (tiles - offset), tiles)
        return pltpu.make_async_remote_copy(
            src_ref=sensors,
            dst_ref=gathered.at[origin],
            send_sem=sensor_send.at[offset],
            recv_sem=sensor_recv.at[offset],
            device_id=sensor_peer(offset),
            device_id_type=MESH,
        )

    def halo_copies(turn):
        copies = []
        for side, (axis, count, place, step) in enumerate(sides):
            way = side % 2
            if turn == 0:
                source, target = (
                    (first_x.at[way], first_x_in.at[1 - way]),
                    (first_y.at[way], first_y_in.at[1 - way]),
                    (
                        base.at[pl.ds(2, 3), pl.ds(way * (cells - rows), rows)],
                        first_z_in.at[1 - way],
                    ),
                )[axis]
            else:
                at = turn - 1
                source, target = (
                    (send_x.at[at, way], recv_x.at[at, 1 - way]),
                    (send_y.at[at, way], recv_y.at[at, 1 - way]),
                    (
                        send_w.at[at, pl.ds(way * (cells - rows), rows)],
                        recv_z.at[at, 1 - way],
                    ),
                )[axis]
            copy = pltpu.make_async_remote_copy(
                src_ref=source,
                dst_ref=target,
                send_sem=halo_send.at[turn, side],
                recv_sem=halo_recv.at[turn, 2 * axis + 1 - way],
                device_id=device_at(axis, step),
                device_id_type=MESH,
            )
            arrival = pltpu.make_async_remote_copy(
                src_ref=source,
                dst_ref=(
                    (first_x_in, first_y_in, first_z_in)[axis].at[way]
                    if turn == 0
                    else (recv_x, recv_y, recv_z)[axis].at[turn - 1, way]
                ),
                send_sem=halo_send.at[turn, side],
                recv_sem=halo_recv.at[turn, side],
                device_id=device_at(axis, step),
                device_id_type=MESH,
            )
            copies.append((inside(count, place, step), copy, arrival))
        return copies

    def start(copies, chosen):
        for side in chosen:
            valid, copy, _ = copies[side]
            pl.when(valid)(copy.start)

    def arrive(copies):
        for valid, _, arrival in copies:
            pl.when(valid)(arrival.wait_recv)

    def sent(copies):
        for valid, copy, _ in copies:
            pl.when(valid)(copy.wait_send)

    copies = halo_copies(0)
    for offset in range(1, tiles):
        sensor_copy(offset).start()
    start(copies, (2, 3, 4, 5, 0, 1))

    full = (cells, cols)
    row_in = lax.rem(lax.broadcasted_iota(jnp.int32, full, 0), rows)
    col_in = lax.broadcasted_iota(jnp.int32, full, 1)
    top, bottom = row_in == 0, row_in == rows - 1
    first_col, last_col = col_in == 0, col_in == cols - 1

    def next_row(array):
        return pltpu.roll(array, cells - 1, 0)

    def prev_row(array):
        return pltpu.roll(array, 1, 0)

    def next_col(array):
        return pltpu.roll(array, cols - 1, 1)

    def prev_col(array):
        return pltpu.roll(array, 1, 1)

    row_next = jnp.where(bottom, 0.0, harmonic(c0, next_row(c0)))
    row_prev = prev_row(row_next)
    col_next = jnp.where(last_col, 0.0, harmonic(c1, next_col(c1)))
    col_prev = prev_col(col_next)
    between = harmonic(c2[: cells - rows], c2[rows:])
    no_layer = jnp.zeros((rows, cols), jnp.float32)
    rate_next_row = jnp.where(bottom, 0.0, next_row(rate))
    rate_prev_row = jnp.where(top, 0.0, prev_row(rate))
    rate_next_col = jnp.where(last_col, 0.0, next_col(rate))
    rate_prev_col = jnp.where(first_col, 0.0, prev_col(rate))
    around = (
        4.0
        - top.astype(jnp.float32)
        - bottom.astype(jnp.float32)
        - first_col.astype(jnp.float32)
        - last_col.astype(jnp.float32)
    )
    stay = 1.0 - around * rate
    turns = jnp.full(full, substeps_ref[x, y])
    inner_faces = (
        row_next
        + row_prev
        + col_next
        + col_prev
        + jnp.concatenate([between, no_layer], axis=0)
        + jnp.concatenate([no_layer, between], axis=0)
    )

    def refine(field):
        for turn in range(MOST_TURNS):
            after = (
                stay * field
                + (rate_next_row * next_row(field) + rate_prev_row * prev_row(field))
                + (rate_next_col * next_col(field) + rate_prev_col * prev_col(field))
            )
            field = jnp.where(turns > turn, after, field)
        return field

    def inner(field, weighted, own):
        return (
            own * field
            + (row_next * next_row(weighted) + row_prev * prev_row(weighted))
            + (col_next * next_col(weighted) + col_prev * prev_col(weighted))
            + jnp.concatenate([between * weighted[rows:], no_layer], axis=0)
            + jnp.concatenate([no_layer, between * weighted[: cells - rows]], axis=0)
        )

    row_key = (me * grid_layers_rows + z * cells).astype(jnp.float32)

    def keys(count, start_at):
        place = lax.broadcasted_iota(jnp.int32, (count, cols), 0).astype(jnp.float32)
        return place + (row_key + start_at)

    arrive(copies)
    for offset in range(1, tiles):
        sensor_arrival(offset).wait_recv()

    row_halo = spread_rows(
        first_x_in[0, 2 * layers : 3 * layers, :], first_x_in[1, 2 * layers : 3 * layers, :]
    )
    row_face = jnp.where(jnp.logical_or(top, bottom), harmonic(c0, row_halo), 0.0)
    packed = first_y_in[0] + first_y_in[1]
    col_halo = unpack_columns(packed, 2 * groups_of_rows)
    col_face = jnp.where(jnp.logical_or(first_col, last_col), harmonic(c1, col_halo), 0.0)
    low_face = harmonic(c2[:rows], first_z_in[0, 0])
    high_face = harmonic(c2[cells - rows :], first_z_in[1, 0])
    middle = cells - 2 * rows

    def with_ends(low, high):
        parts = [low]
        if middle > 0:
            parts.append(jnp.zeros((middle, cols), jnp.float32))
        return jnp.concatenate(parts + [high], axis=0)

    all_faces = inner_faces + row_face + col_face + with_ends(low_face, high_face)
    own = 1.0 - ratio * all_faces

    def outer(row_values, col_values, low_values, high_values):
        return (
            row_face * row_values
            + col_face * col_values
            + with_ends(low_face * low_values, high_face * high_values)
        )

    blocks = []
    folded = max(1, tiles // per)
    for block in range(folded):
        total = gathered[block * per]
        for slot in range(1, per):
            total = total + gathered[block * per + slot]
        blocks.append(total)
    key_rows = [total[steps : steps + 1, :] for total in blocks]
    col_rows = [total[steps + 1 : steps + 2, :] for total in blocks]
    split = [pieces_of(total[0:steps, :]) for total in blocks]
    col_ids = lax.broadcasted_iota(jnp.int32, (cols, cols), 0).astype(jnp.float32)
    in_column = jnp.concatenate(
        [jnp.where(col_ids == line, 1.0, 0.0).astype(jnp.bfloat16) for line in col_rows], axis=1
    )

    def placed(row_keys, sensor_keys, step, piece):
        return jnp.concatenate(
            [
                jnp.where(
                    row_keys == line, parts[piece][step : step + 1, :], 0.0
                ).astype(jnp.bfloat16)
                for line, parts in zip(sensor_keys, split)
            ],
            axis=1,
        )

    def source_of(row_keys, sensor_keys, columns, step):
        total = None
        for piece in range(3):
            part = lax.dot_general(
                placed(row_keys, sensor_keys, step, piece),
                columns,
                NT,
                preferred_element_type=jnp.float32,
            )
            total = part if total is None else total + part
        return total

    last = steps - 1
    own_keys = keys(cells, 0.0)
    level_of = lax.broadcasted_iota(jnp.int32, (2 * layers, cols), 0)
    beside = (ny * grid_layers_rows)
    side_keys = row_key + jnp.where(
        level_of < layers,
        level_of * rows + (rows - 1 - beside),
        (level_of - layers) * rows + beside,
    ).astype(jnp.float32)
    wide_keys = jnp.concatenate(
        [
            own_keys,
            keys(rows, -float(rows)),
            keys(rows, float(cells)),
            side_keys,
            jnp.full((2 * layers, cols), -1.0, jnp.float32),
        ],
        axis=0,
    )
    wide = source_of(wide_keys, key_rows, in_column, last)
    far = float(tiles * grid_layers_rows * 4)
    moved_keys = [
        jnp.where(
            col_line == cols - 1.0,
            key_line + float(grid_layers_rows),
            jnp.where(col_line == 0.0, key_line - float(grid_layers_rows), -far),
        )
        for key_line, col_line in zip(key_rows, col_rows)
    ]
    at_edges = jnp.concatenate(
        [
            jnp.where(
                jnp.logical_or(
                    jnp.logical_and(col_ids == 0.0, line == cols - 1.0),
                    jnp.logical_and(col_ids == cols - 1.0, line == 0.0),
                ),
                1.0,
                0.0,
            ).astype(jnp.bfloat16)
            for line in col_rows
        ],
        axis=1,
    )
    edge = source_of(own_keys, moved_keys, at_edges, last)
    next_source = source_of(own_keys, key_rows, in_column, last - 1)

    field = adjoint + wide[:cells]
    low_src = wide[cells : cells + rows]
    high_src = wide[cells + rows : cells + 2 * rows]
    side_src = wide[cells + 2 * rows : cells + 2 * rows + 2 * layers]
    rows_low = first_x_in[0, layers : 2 * layers, :] * (
        first_x_in[0, 0:layers, :] + side_src[:layers]
    )
    rows_high = first_x_in[1, layers : 2 * layers, :] * (
        first_x_in[1, 0:layers, :] + side_src[layers:]
    )
    cols_adjoint = unpack_columns(packed, 0)
    cols_ratio = unpack_columns(packed, groups_of_rows)
    field = inner(field, ratio * field, own) + outer(
        spread_rows(rows_low, rows_high),
        cols_ratio * (cols_adjoint + edge),
        first_z_in[0, 2] * (first_z_in[0, 1] + low_src),
        first_z_in[1, 2] * (first_z_in[1, 1] + high_src),
    )
    field = refine(field)
    sens = ratio * field

    pending = [copies]
    sources = {last - 1: next_source}
    for turn in range(1, steps):
        step = last - turn
        field = field + sources[step]
        weighted = ratio * field
        copies = halo_copies(turn)
        at = turn - 1
        send_w[at] = weighted
        start(copies, (4, 5))
        left, right = pack_columns((weighted,))
        send_y[at, 0] = left
        send_y[at, 1] = right
        start(copies, (2, 3))
        send_x[at, 0, 0:layers, :] = pick_rows(weighted, 0)
        send_x[at, 1, 0:layers, :] = pick_rows(weighted, rows - 1)
        start(copies, (0, 1))
        pending.append(copies)
        field = inner(field, weighted, own)
        if step > 0:
            sources[step - 1] = source_of(own_keys, key_rows, in_column, step - 1)
        arrive(copies)
        field = field + outer(
            spread_rows(recv_x[at, 0, 0:layers, :], recv_x[at, 1, 0:layers, :]),
            unpack_columns(recv_y[at, 0] + recv_y[at, 1], 0),
            recv_z[at, 0],
            recv_z[at, 1],
        )
        field = refine(field)
        sens = sens + ratio * field

    adjoint_out[...] = field
    sens_out[...] = sens
    for offset in range(1, tiles):
        sensor_copy(offset).wait_send()
    for copies in pending:
        sent(copies)


def solution(mesh):
    nx, ny, nz = mesh.shape["gx"], mesh.shape["gy"], mesh.shape["gz"]
    tiles = nx * ny

    def body(
        adjoint_final,
        conductivity,
        step_ratio,
        refine_rate,
        residual,
        sensor_tile,
        sensor_cell,
        substeps,
    ):
        layers, rows, cols = adjoint_final.shape
        steps, listed = residual.shape
        cells = layers * rows
        flat = (cells, cols)
        wide = -(-3 * layers // SUB) * SUB
        narrow = -(-layers // SUB) * SUB
        height = -(-(steps + 2) // SUB) * SUB
        turns = steps - 1
        f32 = jnp.float32
        hbm = pl.BlockSpec(memory_space=pl.ANY)
        vmem = pl.BlockSpec(memory_space=pltpu.VMEM)
        adjoint, sens = pl.pallas_call(
            functools.partial(kernel, (nx, ny, nz, layers, rows, cols, steps, listed)),
            out_shape=[jax.ShapeDtypeStruct(flat, f32)] * 2,
            in_specs=[hbm] * 7 + [pl.BlockSpec(memory_space=pltpu.SMEM)],
            out_specs=[vmem, vmem],
            scratch_shapes=[
                pltpu.VMEM((6, cells, cols), f32),
                pltpu.VMEM((steps, listed), f32),
                pltpu.VMEM((1, listed), jnp.int32),
                pltpu.VMEM((1, listed), jnp.int32),
                pltpu.VMEM((height, cols), f32),
                pltpu.VMEM((tiles, height, cols), f32),
                pltpu.VMEM((2, wide, cols), f32),
                pltpu.VMEM((2, wide, cols), f32),
                pltpu.VMEM((2, SUB, cols), f32),
                pltpu.VMEM((2, SUB, cols), f32),
                pltpu.VMEM((2, 3, rows, cols), f32),
                pltpu.VMEM((turns, cells, cols), f32),
                pltpu.VMEM((turns, 2, narrow, cols), f32),
                pltpu.VMEM((turns, 2, narrow, cols), f32),
                pltpu.VMEM((turns, 2, SUB, cols), f32),
                pltpu.VMEM((turns, 2, SUB, cols), f32),
                pltpu.VMEM((turns, 2, rows, cols), f32),
                pltpu.SemaphoreType.DMA((7,)),
                pltpu.SemaphoreType.DMA((tiles,)),
                pltpu.SemaphoreType.DMA((tiles,)),
                pltpu.SemaphoreType.DMA((steps, 6)),
                pltpu.SemaphoreType.DMA((steps, 6)),
            ],
            compiler_params=pltpu.CompilerParams(
                collective_id=0, has_side_effects=True, vmem_limit_bytes=32 * 1024 * 1024
            ),
        )(
            conductivity.reshape(3, *flat),
            adjoint_final.reshape(flat),
            step_ratio.reshape(flat),
            refine_rate.reshape(flat),
            residual,
            sensor_tile.reshape(1, listed),
            sensor_cell.reshape(1, listed),
            substeps,
        )
        return adjoint.reshape(layers, rows, cols), sens.reshape(layers, rows, cols)

    return jax.shard_map(
        body,
        mesh=mesh,
        in_specs=(
            P("gz", "gx", "gy"),
            P(None, "gz", "gx", "gy"),
            P("gz", "gx", "gy"),
            P("gz", "gx", "gy"),
            P(None, ("gx", "gy")),
            P(("gx", "gy")),
            P(("gx", "gy")),
            P(),
        ),
        out_specs=(P("gz", "gx", "gy"), P("gz", "gx", "gy")),
        check_vma=False,
    )
```

```python
import functools

import jax
import jax.numpy as jnp
from jax import lax
from jax.experimental import pallas as pl
from jax.experimental.pallas import tpu as pltpu
from jax.sharding import PartitionSpec as P

MESH = pl.DeviceIdType.MESH
MOST_TURNS = 6
SUB = 8
NT = (((1,), (1,)), ((), ()))


def harmonic(first, second):
    return 2.0 * first * second / (first + second)


def pieces_of(values):
    high = values.astype(jnp.bfloat16).astype(jnp.float32)
    rest = values - high
    middle = rest.astype(jnp.bfloat16).astype(jnp.float32)
    return high, middle, rest - middle


def kernel(
    sizes,
    cond_hbm,
    adjoint_hbm,
    ratio_hbm,
    rate_hbm,
    res_hbm,
    tile_hbm,
    cell_hbm,
    substeps_hbm,
    adjoint_out,
    sens_out,
    base,
    res_in,
    tile_in,
    cell_in,
    substeps_ref,
    sensors,
    gathered,
    first_x,
    first_x_in,
    first_y,
    first_y_in,
    first_z_in,
    send_w,
    send_x,
    recv_x,
    send_y,
    recv_y,
    recv_z,
    results,
    load_sem,
    store_sem,
    sensor_send,
    sensor_recv,
    halo_send,
    halo_recv,
):
    nx, ny, nz, layers, rows, cols, steps, listed = sizes
    cells = layers * rows
    groups_of_rows = cells // SUB
    tiles = nx * ny
    x, y, z = lax.axis_index("gx"), lax.axis_index("gy"), lax.axis_index("gz")
    me = x * ny + y

    loads = [
        pltpu.make_async_copy(src, dst, load_sem.at[k])
        for k, (src, dst) in enumerate(
            (
                (res_hbm, res_in),
                (tile_hbm, tile_in),
                (cell_hbm, cell_in),
                (adjoint_hbm, base.at[3]),
                (ratio_hbm, base.at[4]),
                (cond_hbm, base.at[pl.ds(0, 3)]),
                (rate_hbm, base.at[5]),
                (substeps_hbm, substeps_ref),
            )
        )
    ]
    for load in loads:
        load.start()

    for ref in (first_x_in, first_y_in, first_z_in, recv_x, recv_y, recv_z, sensors):
        ref[...] = jnp.zeros_like(ref)

    sides = (
        (0, nx, x, -1),
        (0, nx, x, 1),
        (1, ny, y, -1),
        (1, ny, y, 1),
        (2, nz, z, -1),
        (2, nz, z, 1),
    )

    def device_at(axis, step):
        place = [x, y, z]
        place[axis] = place[axis] + step
        return tuple(place)

    def inside(count, place, step):
        return place > 0 if step < 0 else place < count - 1

    barrier = pltpu.get_barrier_semaphore()

    def sensor_peer(offset):
        there = lax.rem(me + offset, tiles)
        return (lax.div(there, ny), lax.rem(there, ny), z)

    for offset in range(1, tiles):
        pl.semaphore_signal(barrier, inc=1, device_id=sensor_peer(offset), device_id_type=MESH)
    for axis, count, place, step in sides[4:]:

        @pl.when(inside(count, place, step))
        def _():
            pl.semaphore_signal(
                barrier, inc=1, device_id=device_at(axis, step), device_id_type=MESH
            )

    for load in loads[:3]:
        load.wait()
    per = max(1, cols // listed)
    lane = lax.broadcasted_iota(jnp.int32, (1, cols), 1)
    cell = cell_in[...]
    grid_layers_rows = nz * cells
    key = tile_in[...] * grid_layers_rows + lax.div(cell, cols)
    column = lax.rem(cell, cols)
    for slot in range(per):
        here = pl.ds(slot * listed, listed)
        sensors[0:steps, here] = res_in[...]
        sensors[steps : steps + 1, here] = key.astype(jnp.float32)
        sensors[steps + 1 : steps + 2, here] = column.astype(jnp.float32)
    if per > 1:
        mine = lax.div(lane, listed) == lax.rem(me, per)
        sensors[...] = jnp.where(mine, sensors[...], 0.0)
    gathered[me] = sensors[...]

    for load in loads[3:]:
        load.wait()
    lanes = lax.broadcasted_iota(jnp.int32, (SUB, cols), 1)

    def pack_columns(arrays):
        to_left = jnp.zeros((SUB, cols), jnp.float32)
        to_right = jnp.zeros((SUB, cols), jnp.float32)
        spot = 0
        for array in arrays:
            for part in range(groups_of_rows):
                block = array[part * SUB : (part + 1) * SUB, :]
                left = pltpu.roll(block, spot % cols, 1)
                right = pltpu.roll(block, (spot + 2) % cols, 1)
                to_left = jnp.where(lanes == spot, left, to_left)
                to_right = jnp.where(lanes == spot + 1, right, to_right)
                spot += 2
        return to_left, to_right

    def unpack_columns(packed, spot):
        return jnp.concatenate(
            [
                pltpu.roll(packed, (cols - 2 * (spot + part) - 1) % cols, 1)
                for part in range(groups_of_rows)
            ],
            axis=0,
        )

    def pick_rows(array, row):
        return jnp.concatenate(
            [array[level * rows + row : level * rows + row + 1, :] for level in range(layers)],
            axis=0,
        )

    def spread_rows(low, high):
        half = rows // 2
        parts = []
        for level in range(layers):
            parts.append(jnp.broadcast_to(low[level : level + 1, :], (half, cols)))
            parts.append(jnp.broadcast_to(high[level : level + 1, :], (rows - half, cols)))
        return jnp.concatenate(parts, axis=0)

    c0, c1, c2 = base[0], base[1], base[2]
    adjoint, ratio, rate = base[3], base[4], base[5]

    for k, array in enumerate((adjoint, ratio, c0)):
        first_x[0, k * layers : (k + 1) * layers, :] = pick_rows(array, 0)
        first_x[1, k * layers : (k + 1) * layers, :] = pick_rows(array, rows - 1)
    left, right = pack_columns((adjoint, ratio, c1))
    first_y[0] = left
    first_y[1] = right

    neighbours = (
        (tiles - 1)
        + (z > 0).astype(jnp.int32)
        + (z < nz - 1).astype(jnp.int32)
    )
    pl.semaphore_wait(barrier, neighbours)

    def sensor_copy(offset):
        return pltpu.make_async_remote_copy(
            src_ref=sensors,
            dst_ref=gathered.at[me],
            send_sem=sensor_send.at[offset],
            recv_sem=sensor_recv.at[offset],
            device_id=sensor_peer(offset),
            device_id_type=MESH,
        )

    def sensor_arrival(offset):
        origin = lax.rem(me + (tiles - offset), tiles)
        return pltpu.make_async_remote_copy(
            src_ref=sensors,
            dst_ref=gathered.at[origin],
            send_sem=sensor_send.at[offset],
            recv_sem=sensor_recv.at[offset],
            device_id=sensor_peer(offset),
            device_id_type=MESH,
        )

    def halo_copies(turn):
        copies = []
        for side, (axis, count, place, step) in enumerate(sides):
            way = side % 2
            if turn == 0:
                source, target = (
                    (first_x.at[way], first_x_in.at[1 - way]),
                    (first_y.at[way], first_y_in.at[1 - way]),
                    (
                        base.at[pl.ds(2, 3), pl.ds(way * (cells - rows), rows)],
                        first_z_in.at[1 - way],
                    ),
                )[axis]
            else:
                at = turn - 1
                source, target = (
                    (send_x.at[at, way], recv_x.at[at, 1 - way]),
                    (send_y.at[at, way], recv_y.at[at, 1 - way]),
                    (
                        send_w.at[at, pl.ds(way * (cells - rows), rows)],
                        recv_z.at[at, 1 - way],
                    ),
                )[axis]
            copy = pltpu.make_async_remote_copy(
                src_ref=source,
                dst_ref=target,
                send_sem=halo_send.at[turn, side],
                recv_sem=halo_recv.at[turn, 2 * axis + 1 - way],
                device_id=device_at(axis, step),
                device_id_type=MESH,
            )
            arrival = pltpu.make_async_remote_copy(
                src_ref=source,
                dst_ref=(
                    (first_x_in, first_y_in, first_z_in)[axis].at[way]
                    if turn == 0
                    else (recv_x, recv_y, recv_z)[axis].at[turn - 1, way]
                ),
                send_sem=halo_send.at[turn, side],
                recv_sem=halo_recv.at[turn, side],
                device_id=device_at(axis, step),
                device_id_type=MESH,
            )
            copies.append((inside(count, place, step), copy, arrival))
        return copies

    def start(copies, chosen):
        for side in chosen:
            valid, copy, _ = copies[side]
            pl.when(valid)(copy.start)

    def arrive(copies):
        for valid, _, arrival in copies:
            pl.when(valid)(arrival.wait_recv)

    def sent(copies):
        for valid, copy, _ in copies:
            pl.when(valid)(copy.wait_send)

    copies = halo_copies(0)
    for offset in range(1, tiles):
        sensor_copy(offset).start()
    start(copies, (2, 3, 4, 5, 0, 1))

    full = (cells, cols)
    row_in = lax.rem(lax.broadcasted_iota(jnp.int32, full, 0), rows)
    col_in = lax.broadcasted_iota(jnp.int32, full, 1)
    top, bottom = row_in == 0, row_in == rows - 1
    first_col, last_col = col_in == 0, col_in == cols - 1

    def next_row(array):
        return pltpu.roll(array, cells - 1, 0)

    def prev_row(array):
        return pltpu.roll(array, 1, 0)

    def next_col(array):
        return pltpu.roll(array, cols - 1, 1)

    def prev_col(array):
        return pltpu.roll(array, 1, 1)

    row_next = jnp.where(bottom, 0.0, harmonic(c0, next_row(c0)))
    row_prev = prev_row(row_next)
    col_next = jnp.where(last_col, 0.0, harmonic(c1, next_col(c1)))
    col_prev = prev_col(col_next)
    between = harmonic(c2[: cells - rows], c2[rows:])
    no_layer = jnp.zeros((rows, cols), jnp.float32)
    rate_next_row = jnp.where(bottom, 0.0, next_row(rate))
    rate_prev_row = jnp.where(top, 0.0, prev_row(rate))
    rate_next_col = jnp.where(last_col, 0.0, next_col(rate))
    rate_prev_col = jnp.where(first_col, 0.0, prev_col(rate))
    around = (
        4.0
        - top.astype(jnp.float32)
        - bottom.astype(jnp.float32)
        - first_col.astype(jnp.float32)
        - last_col.astype(jnp.float32)
    )
    stay = 1.0 - around * rate
    turns = jnp.full(full, substeps_ref[x, y])
    inner_faces = (
        row_next
        + row_prev
        + col_next
        + col_prev
        + jnp.concatenate([between, no_layer], axis=0)
        + jnp.concatenate([no_layer, between], axis=0)
    )

    def refine(field):
        for turn in range(MOST_TURNS):
            after = (
                stay * field
                + (rate_next_row * next_row(field) + rate_prev_row * prev_row(field))
                + (rate_next_col * next_col(field) + rate_prev_col * prev_col(field))
            )
            field = jnp.where(turns > turn, after, field)
        return field

    def inner(field, weighted, own):
        return (
            own * field
            + (row_next * next_row(weighted) + row_prev * prev_row(weighted))
            + (col_next * next_col(weighted) + col_prev * prev_col(weighted))
            + jnp.concatenate([between * weighted[rows:], no_layer], axis=0)
            + jnp.concatenate([no_layer, between * weighted[: cells - rows]], axis=0)
        )

    row_key = (me * grid_layers_rows + z * cells).astype(jnp.float32)

    def keys(count, start_at):
        place = lax.broadcasted_iota(jnp.int32, (count, cols), 0).astype(jnp.float32)
        return place + (row_key + start_at)

    arrive(copies)
    for offset in range(1, tiles):
        sensor_arrival(offset).wait_recv()

    row_halo = spread_rows(
        first_x_in[0, 2 * layers : 3 * layers, :], first_x_in[1, 2 * layers : 3 * layers, :]
    )
    row_face = jnp.where(jnp.logical_or(top, bottom), harmonic(c0, row_halo), 0.0)
    packed = first_y_in[0] + first_y_in[1]
    col_halo = unpack_columns(packed, 2 * groups_of_rows)
    col_face = jnp.where(jnp.logical_or(first_col, last_col), harmonic(c1, col_halo), 0.0)
    low_face = harmonic(c2[:rows], first_z_in[0, 0])
    high_face = harmonic(c2[cells - rows :], first_z_in[1, 0])
    middle = cells - 2 * rows

    def with_ends(low, high):
        parts = [low]
        if middle > 0:
            parts.append(jnp.zeros((middle, cols), jnp.float32))
        return jnp.concatenate(parts + [high], axis=0)

    all_faces = inner_faces + row_face + col_face + with_ends(low_face, high_face)
    own = 1.0 - ratio * all_faces

    def outer(row_values, col_values, low_values, high_values):
        return (
            row_face * row_values
            + col_face * col_values
            + with_ends(low_face * low_values, high_face * high_values)
        )

    blocks = []
    folded = max(1, tiles // per)
    for block in range(folded):
        total = gathered[block * per]
        for slot in range(1, per):
            total = total + gathered[block * per + slot]
        blocks.append(total)
    key_rows = [total[steps : steps + 1, :] for total in blocks]
    col_rows = [total[steps + 1 : steps + 2, :] for total in blocks]
    split = [pieces_of(total[0:steps, :]) for total in blocks]
    col_ids = lax.broadcasted_iota(jnp.int32, (cols, cols), 0).astype(jnp.float32)
    in_column = jnp.concatenate(
        [jnp.where(col_ids == line, 1.0, 0.0).astype(jnp.bfloat16) for line in col_rows], axis=1
    )

    def placed(row_keys, sensor_keys, step, piece):
        return jnp.concatenate(
            [
                jnp.where(
                    row_keys == line, parts[piece][step : step + 1, :], 0.0
                ).astype(jnp.bfloat16)
                for line, parts in zip(sensor_keys, split)
            ],
            axis=1,
        )

    def source_of(row_keys, sensor_keys, columns, step):
        total = None
        for piece in range(3):
            part = lax.dot_general(
                placed(row_keys, sensor_keys, step, piece),
                columns,
                NT,
                preferred_element_type=jnp.float32,
            )
            total = part if total is None else total + part
        return total

    last = steps - 1
    own_keys = keys(cells, 0.0)
    level_of = lax.broadcasted_iota(jnp.int32, (2 * layers, cols), 0)
    beside = (ny * grid_layers_rows)
    side_keys = row_key + jnp.where(
        level_of < layers,
        level_of * rows + (rows - 1 - beside),
        (level_of - layers) * rows + beside,
    ).astype(jnp.float32)
    wide_keys = jnp.concatenate(
        [
            own_keys,
            keys(rows, -float(rows)),
            keys(rows, float(cells)),
            side_keys,
            jnp.full((2 * layers, cols), -1.0, jnp.float32),
        ],
        axis=0,
    )
    wide = source_of(wide_keys, key_rows, in_column, last)
    far = float(tiles * grid_layers_rows * 4)
    moved_keys = [
        jnp.where(
            col_line == cols - 1.0,
            key_line + float(grid_layers_rows),
            jnp.where(col_line == 0.0, key_line - float(grid_layers_rows), -far),
        )
        for key_line, col_line in zip(key_rows, col_rows)
    ]
    at_edges = jnp.concatenate(
        [
            jnp.where(
                jnp.logical_or(
                    jnp.logical_and(col_ids == 0.0, line == cols - 1.0),
                    jnp.logical_and(col_ids == cols - 1.0, line == 0.0),
                ),
                1.0,
                0.0,
            ).astype(jnp.bfloat16)
            for line in col_rows
        ],
        axis=1,
    )
    edge = source_of(own_keys, moved_keys, at_edges, last)
    next_source = source_of(own_keys, key_rows, in_column, last - 1)

    field = adjoint + wide[:cells]
    low_src = wide[cells : cells + rows]
    high_src = wide[cells + rows : cells + 2 * rows]
    side_src = wide[cells + 2 * rows : cells + 2 * rows + 2 * layers]
    rows_low = first_x_in[0, layers : 2 * layers, :] * (
        first_x_in[0, 0:layers, :] + side_src[:layers]
    )
    rows_high = first_x_in[1, layers : 2 * layers, :] * (
        first_x_in[1, 0:layers, :] + side_src[layers:]
    )
    cols_adjoint = unpack_columns(packed, 0)
    cols_ratio = unpack_columns(packed, groups_of_rows)
    field = inner(field, ratio * field, own) + outer(
        spread_rows(rows_low, rows_high),
        cols_ratio * (cols_adjoint + edge),
        first_z_in[0, 2] * (first_z_in[0, 1] + low_src),
        first_z_in[1, 2] * (first_z_in[1, 1] + high_src),
    )
    field = refine(field)
    sens = ratio * field

    pending = [copies]
    sources = {last - 1: next_source}
    for turn in range(1, steps):
        step = last - turn
        field = field + sources[step]
        weighted = ratio * field
        copies = halo_copies(turn)
        at = turn - 1
        send_w[at] = weighted
        start(copies, (4, 5))
        left, right = pack_columns((weighted,))
        send_y[at, 0] = left
        send_y[at, 1] = right
        start(copies, (2, 3))
        send_x[at, 0, 0:layers, :] = pick_rows(weighted, 0)
        send_x[at, 1, 0:layers, :] = pick_rows(weighted, rows - 1)
        start(copies, (0, 1))
        pending.append(copies)
        field = inner(field, weighted, own)
        if step > 0:
            sources[step - 1] = source_of(own_keys, key_rows, in_column, step - 1)
        arrive(copies)
        field = field + outer(
            spread_rows(recv_x[at, 0, 0:layers, :], recv_x[at, 1, 0:layers, :]),
            unpack_columns(recv_y[at, 0] + recv_y[at, 1], 0),
            recv_z[at, 0],
            recv_z[at, 1],
        )
        field = refine(field)
        sens = sens + ratio * field

    results[0] = field
    results[1] = sens
    stores = [
        pltpu.make_async_copy(results.at[k], out, store_sem.at[k])
        for k, out in enumerate((adjoint_out, sens_out))
    ]
    for store in stores:
        store.start()
    for offset in range(1, tiles):
        sensor_copy(offset).wait_send()
    for copies in pending:
        sent(copies)
    for store in stores:
        store.wait()


def deliver(first, second, first_out, second_out, sems):
    copies = (
        pltpu.make_async_copy(first, first_out, sems.at[0]),
        pltpu.make_async_copy(second, second_out, sems.at[1]),
    )
    for copy in copies:
        copy.start()
    for copy in copies:
        copy.wait()


def solution(mesh):
    nx, ny, nz = mesh.shape["gx"], mesh.shape["gy"], mesh.shape["gz"]
    tiles = nx * ny

    def body(
        adjoint_final,
        conductivity,
        step_ratio,
        refine_rate,
        residual,
        sensor_tile,
        sensor_cell,
        substeps,
    ):
        layers, rows, cols = adjoint_final.shape
        steps, listed = residual.shape
        cells = layers * rows
        flat = (cells, cols)
        wide = -(-3 * layers // SUB) * SUB
        narrow = -(-layers // SUB) * SUB
        height = -(-(steps + 2) // SUB) * SUB
        turns = steps - 1
        f32 = jnp.float32
        hbm = pl.BlockSpec(memory_space=pltpu.HBM)
        adjoint, sens = pl.pallas_call(
            functools.partial(kernel, (nx, ny, nz, layers, rows, cols, steps, listed)),
            out_shape=[jax.ShapeDtypeStruct(flat, f32)] * 2,
            in_specs=[hbm] * 8,
            out_specs=[hbm, hbm],
            scratch_shapes=[
                pltpu.VMEM((6, cells, cols), f32),
                pltpu.VMEM((steps, listed), f32),
                pltpu.VMEM((1, listed), jnp.int32),
                pltpu.VMEM((1, listed), jnp.int32),
                pltpu.SMEM(substeps.shape, jnp.int32),
                pltpu.VMEM((height, cols), f32),
                pltpu.VMEM((tiles, height, cols), f32),
                pltpu.VMEM((2, wide, cols), f32),
                pltpu.VMEM((2, wide, cols), f32),
                pltpu.VMEM((2, SUB, cols), f32),
                pltpu.VMEM((2, SUB, cols), f32),
                pltpu.VMEM((2, 3, rows, cols), f32),
                pltpu.VMEM((turns, cells, cols), f32),
                pltpu.VMEM((turns, 2, narrow, cols), f32),
                pltpu.VMEM((turns, 2, narrow, cols), f32),
                pltpu.VMEM((turns, 2, SUB, cols), f32),
                pltpu.VMEM((turns, 2, SUB, cols), f32),
                pltpu.VMEM((turns, 2, rows, cols), f32),
                pltpu.VMEM((2, cells, cols), f32),
                pltpu.SemaphoreType.DMA((8,)),
                pltpu.SemaphoreType.DMA((2,)),
                pltpu.SemaphoreType.DMA((tiles,)),
                pltpu.SemaphoreType.DMA((tiles,)),
                pltpu.SemaphoreType.DMA((steps, 6)),
                pltpu.SemaphoreType.DMA((steps, 6)),
            ],
            compiler_params=pltpu.CompilerParams(
                collective_id=0, has_side_effects=True, vmem_limit_bytes=63 * 1024 * 1024
            ),
        )(
            conductivity.reshape(3, *flat),
            adjoint_final.reshape(flat),
            step_ratio.reshape(flat),
            refine_rate.reshape(flat),
            residual,
            sensor_tile.reshape(1, listed),
            sensor_cell.reshape(1, listed),
            substeps,
        )
        adjoint, sens = pl.pallas_call(
            deliver,
            out_shape=[jax.ShapeDtypeStruct(flat, f32)] * 2,
            in_specs=[hbm, hbm],
            out_specs=[hbm, hbm],
            scratch_shapes=[pltpu.SemaphoreType.DMA((2,))],
            compiler_params=pltpu.CompilerParams(vmem_limit_bytes=63 * 1024 * 1024),
        )(adjoint, sens)
        return adjoint.reshape(layers, rows, cols), sens.reshape(layers, rows, cols)

    return jax.shard_map(
        body,
        mesh=mesh,
        in_specs=(
            P("gz", "gx", "gy"),
            P(None, "gz", "gx", "gy"),
            P("gz", "gx", "gy"),
            P("gz", "gx", "gy"),
            P(None, ("gx", "gy")),
            P(("gx", "gy")),
            P(("gx", "gy")),
            P(),
        ),
        out_specs=(P("gz", "gx", "gy"), P("gz", "gx", "gy")),
        check_vma=False,
    )
```

```python
import functools

import jax
import jax.numpy as jnp
from jax import lax
from jax.experimental import pallas as pl
from jax.experimental.pallas import tpu as pltpu
from jax.sharding import PartitionSpec as P

MESH = pl.DeviceIdType.MESH
MOST_TURNS = 6
SUB = 8
NT = (((1,), (1,)), ((), ()))


def harmonic(first, second):
    return 2.0 * first * second / (first + second)


def pieces_of(values):
    high = values.astype(jnp.bfloat16).astype(jnp.float32)
    rest = values - high
    middle = rest.astype(jnp.bfloat16).astype(jnp.float32)
    return high, middle, rest - middle


def kernel(
    sizes,
    cond_hbm,
    adjoint_hbm,
    ratio_hbm,
    rate_hbm,
    res_hbm,
    tile_hbm,
    cell_hbm,
    substeps_hbm,
    adjoint_out,
    sens_out,
    base,
    res_in,
    tile_in,
    cell_in,
    substeps_ref,
    sensors,
    gathered,
    first_x,
    first_x_in,
    first_y,
    first_y_in,
    first_z_in,
    send_w,
    send_x,
    recv_x,
    send_y,
    recv_y,
    recv_z,
    sources,
    load_sem,
    sensor_send,
    sensor_recv,
    halo_send,
    halo_recv,
):
    nx, ny, nz, layers, rows, cols, steps, listed = sizes
    cells = layers * rows
    groups_of_rows = cells // SUB
    tiles = nx * ny
    x, y, z = lax.axis_index("gx"), lax.axis_index("gy"), lax.axis_index("gz")
    me = x * ny + y

    loads = [
        pltpu.make_async_copy(src, dst, load_sem.at[k])
        for k, (src, dst) in enumerate(
            (
                (res_hbm, res_in),
                (tile_hbm, tile_in),
                (cell_hbm, cell_in),
                (adjoint_hbm, base.at[3]),
                (ratio_hbm, base.at[4]),
                (cond_hbm, base.at[pl.ds(0, 3)]),
                (rate_hbm, base.at[5]),
                (substeps_hbm, substeps_ref),
            )
        )
    ]
    for load in loads:
        load.start()

    for ref in (first_x_in, first_y_in, first_z_in, recv_x, recv_y, recv_z, sensors):
        ref[...] = jnp.zeros_like(ref)

    sides = (
        (0, nx, x, -1),
        (0, nx, x, 1),
        (1, ny, y, -1),
        (1, ny, y, 1),
        (2, nz, z, -1),
        (2, nz, z, 1),
    )

    def device_at(axis, step):
        place = [x, y, z]
        place[axis] = place[axis] + step
        return tuple(place)

    def inside(count, place, step):
        return place > 0 if step < 0 else place < count - 1

    barrier = pltpu.get_barrier_semaphore()

    def sensor_peer(offset):
        there = lax.rem(me + offset, tiles)
        return (lax.div(there, ny), lax.rem(there, ny), z)

    for offset in range(1, tiles):
        pl.semaphore_signal(barrier, inc=1, device_id=sensor_peer(offset), device_id_type=MESH)
    for axis, count, place, step in sides[4:]:

        @pl.when(inside(count, place, step))
        def _():
            pl.semaphore_signal(
                barrier, inc=1, device_id=device_at(axis, step), device_id_type=MESH
            )

    for load in loads[:3]:
        load.wait()
    per = max(1, cols // listed)
    lane = lax.broadcasted_iota(jnp.int32, (1, cols), 1)
    cell = cell_in[...]
    grid_layers_rows = nz * cells
    key = tile_in[...] * grid_layers_rows + lax.div(cell, cols)
    column = lax.rem(cell, cols)
    for slot in range(per):
        here = pl.ds(slot * listed, listed)
        sensors[0:steps, here] = res_in[...]
        sensors[steps : steps + 1, here] = key.astype(jnp.float32)
        sensors[steps + 1 : steps + 2, here] = column.astype(jnp.float32)
    if per > 1:
        mine = lax.div(lane, listed) == lax.rem(me, per)
        sensors[...] = jnp.where(mine, sensors[...], 0.0)
    gathered[me] = sensors[...]

    for load in loads[3:]:
        load.wait()
    lanes = lax.broadcasted_iota(jnp.int32, (SUB, cols), 1)

    def pack_columns(arrays):
        to_left = jnp.zeros((SUB, cols), jnp.float32)
        to_right = jnp.zeros((SUB, cols), jnp.float32)
        spot = 0
        for array in arrays:
            for part in range(groups_of_rows):
                block = array[part * SUB : (part + 1) * SUB, :]
                left = pltpu.roll(block, spot % cols, 1)
                right = pltpu.roll(block, (spot + 2) % cols, 1)
                to_left = jnp.where(lanes == spot, left, to_left)
                to_right = jnp.where(lanes == spot + 1, right, to_right)
                spot += 2
        return to_left, to_right

    def unpack_columns(packed, spot):
        return jnp.concatenate(
            [
                pltpu.roll(packed, (cols - 2 * (spot + part) - 1) % cols, 1)
                for part in range(groups_of_rows)
            ],
            axis=0,
        )

    def pick_rows(array, row):
        return jnp.concatenate(
            [array[level * rows + row : level * rows + row + 1, :] for level in range(layers)],
            axis=0,
        )

    def spread_rows(low, high):
        half = rows // 2
        parts = []
        for level in range(layers):
            parts.append(jnp.broadcast_to(low[level : level + 1, :], (half, cols)))
            parts.append(jnp.broadcast_to(high[level : level + 1, :], (rows - half, cols)))
        return jnp.concatenate(parts, axis=0)

    c0, c1, c2 = base[0], base[1], base[2]
    adjoint, ratio, rate = base[3], base[4], base[5]

    for k, array in enumerate((adjoint, ratio, c0)):
        first_x[0, k * layers : (k + 1) * layers, :] = pick_rows(array, 0)
        first_x[1, k * layers : (k + 1) * layers, :] = pick_rows(array, rows - 1)
    left, right = pack_columns((adjoint, ratio, c1))
    first_y[0] = left
    first_y[1] = right

    neighbours = (
        (tiles - 1)
        + (z > 0).astype(jnp.int32)
        + (z < nz - 1).astype(jnp.int32)
    )
    pl.semaphore_wait(barrier, neighbours)

    def sensor_copy(offset):
        return pltpu.make_async_remote_copy(
            src_ref=sensors,
            dst_ref=gathered.at[me],
            send_sem=sensor_send.at[offset],
            recv_sem=sensor_recv.at[offset],
            device_id=sensor_peer(offset),
            device_id_type=MESH,
        )

    def sensor_arrival(offset):
        origin = lax.rem(me + (tiles - offset), tiles)
        return pltpu.make_async_remote_copy(
            src_ref=sensors,
            dst_ref=gathered.at[origin],
            send_sem=sensor_send.at[offset],
            recv_sem=sensor_recv.at[offset],
            device_id=sensor_peer(offset),
            device_id_type=MESH,
        )

    def halo_copies(turn):
        copies = []
        first = isinstance(turn, int) and turn == 0
        for side, (axis, count, place, step) in enumerate(sides):
            way = side % 2
            if first:
                source, target = (
                    (first_x.at[way], first_x_in.at[1 - way]),
                    (first_y.at[way], first_y_in.at[1 - way]),
                    (
                        base.at[pl.ds(2, 3), pl.ds(way * (cells - rows), rows)],
                        first_z_in.at[1 - way],
                    ),
                )[axis]
            else:
                at = turn - 1
                source, target = (
                    (send_x.at[at, way], recv_x.at[at, 1 - way]),
                    (send_y.at[at, way], recv_y.at[at, 1 - way]),
                    (
                        send_w.at[at, pl.ds(way * (cells - rows), rows)],
                        recv_z.at[at, 1 - way],
                    ),
                )[axis]
            copy = pltpu.make_async_remote_copy(
                src_ref=source,
                dst_ref=target,
                send_sem=halo_send.at[turn, side],
                recv_sem=halo_recv.at[turn, 2 * axis + 1 - way],
                device_id=device_at(axis, step),
                device_id_type=MESH,
            )
            arrival = pltpu.make_async_remote_copy(
                src_ref=source,
                dst_ref=(
                    (first_x_in, first_y_in, first_z_in)[axis].at[way]
                    if first
                    else (recv_x, recv_y, recv_z)[axis].at[turn - 1, way]
                ),
                send_sem=halo_send.at[turn, side],
                recv_sem=halo_recv.at[turn, side],
                device_id=device_at(axis, step),
                device_id_type=MESH,
            )
            copies.append((inside(count, place, step), copy, arrival))
        return copies

    def start(copies, chosen):
        for side in chosen:
            valid, copy, _ = copies[side]
            pl.when(valid)(copy.start)

    def arrive(copies):
        for valid, _, arrival in copies:
            pl.when(valid)(arrival.wait_recv)

    def sent(copies):
        for valid, copy, _ in copies:
            pl.when(valid)(copy.wait_send)

    copies = halo_copies(0)
    for offset in range(1, tiles):
        sensor_copy(offset).start()
    start(copies, (2, 3, 4, 5, 0, 1))

    full = (cells, cols)
    row_in = lax.rem(lax.broadcasted_iota(jnp.int32, full, 0), rows)
    col_in = lax.broadcasted_iota(jnp.int32, full, 1)
    top, bottom = row_in == 0, row_in == rows - 1
    first_col, last_col = col_in == 0, col_in == cols - 1

    def next_row(array):
        return pltpu.roll(array, cells - 1, 0)

    def prev_row(array):
        return pltpu.roll(array, 1, 0)

    def next_col(array):
        return pltpu.roll(array, cols - 1, 1)

    def prev_col(array):
        return pltpu.roll(array, 1, 1)

    row_next = jnp.where(bottom, 0.0, harmonic(c0, next_row(c0)))
    row_prev = prev_row(row_next)
    col_next = jnp.where(last_col, 0.0, harmonic(c1, next_col(c1)))
    col_prev = prev_col(col_next)
    between = harmonic(c2[: cells - rows], c2[rows:])
    no_layer = jnp.zeros((rows, cols), jnp.float32)
    rate_next_row = jnp.where(bottom, 0.0, next_row(rate))
    rate_prev_row = jnp.where(top, 0.0, prev_row(rate))
    rate_next_col = jnp.where(last_col, 0.0, next_col(rate))
    rate_prev_col = jnp.where(first_col, 0.0, prev_col(rate))
    around = (
        4.0
        - top.astype(jnp.float32)
        - bottom.astype(jnp.float32)
        - first_col.astype(jnp.float32)
        - last_col.astype(jnp.float32)
    )
    stay = 1.0 - around * rate
    turns = jnp.full(full, substeps_ref[x, y])
    inner_faces = (
        row_next
        + row_prev
        + col_next
        + col_prev
        + jnp.concatenate([between, no_layer], axis=0)
        + jnp.concatenate([no_layer, between], axis=0)
    )

    def refine(field):
        def one_turn(turn, field):
            after = (
                stay * field
                + (rate_next_row * next_row(field) + rate_prev_row * prev_row(field))
                + (rate_next_col * next_col(field) + rate_prev_col * prev_col(field))
            )
            return jnp.where(turns > turn, after, field)

        return lax.fori_loop(0, MOST_TURNS, one_turn, field)

    def inner(field, weighted, own):
        return (
            own * field
            + (row_next * next_row(weighted) + row_prev * prev_row(weighted))
            + (col_next * next_col(weighted) + col_prev * prev_col(weighted))
            + jnp.concatenate([between * weighted[rows:], no_layer], axis=0)
            + jnp.concatenate([no_layer, between * weighted[: cells - rows]], axis=0)
        )

    row_key = (me * grid_layers_rows + z * cells).astype(jnp.float32)

    def keys(count, start_at):
        place = lax.broadcasted_iota(jnp.int32, (count, cols), 0).astype(jnp.float32)
        return place + (row_key + start_at)

    arrive(copies)
    for offset in range(1, tiles):
        sensor_arrival(offset).wait_recv()

    row_halo = spread_rows(
        first_x_in[0, 2 * layers : 3 * layers, :], first_x_in[1, 2 * layers : 3 * layers, :]
    )
    row_face = jnp.where(jnp.logical_or(top, bottom), harmonic(c0, row_halo), 0.0)
    packed = first_y_in[0] + first_y_in[1]
    col_halo = unpack_columns(packed, 2 * groups_of_rows)
    col_face = jnp.where(jnp.logical_or(first_col, last_col), harmonic(c1, col_halo), 0.0)
    low_face = harmonic(c2[:rows], first_z_in[0, 0])
    high_face = harmonic(c2[cells - rows :], first_z_in[1, 0])
    middle = cells - 2 * rows

    def with_ends(low, high):
        parts = [low]
        if middle > 0:
            parts.append(jnp.zeros((middle, cols), jnp.float32))
        return jnp.concatenate(parts + [high], axis=0)

    all_faces = inner_faces + row_face + col_face + with_ends(low_face, high_face)
    own = 1.0 - ratio * all_faces

    def outer(row_values, col_values, low_values, high_values):
        return (
            row_face * row_values
            + col_face * col_values
            + with_ends(low_face * low_values, high_face * high_values)
        )

    blocks = []
    folded = max(1, tiles // per)
    for block in range(folded):
        total = gathered[block * per]
        for slot in range(1, per):
            total = total + gathered[block * per + slot]
        blocks.append(total)
    key_rows = [total[steps : steps + 1, :] for total in blocks]
    col_rows = [total[steps + 1 : steps + 2, :] for total in blocks]
    split = [pieces_of(total[0:steps, :]) for total in blocks]
    col_ids = lax.broadcasted_iota(jnp.int32, (cols, cols), 0).astype(jnp.float32)
    in_column = jnp.concatenate(
        [jnp.where(col_ids == line, 1.0, 0.0).astype(jnp.bfloat16) for line in col_rows], axis=1
    )

    def placed(row_keys, sensor_keys, step, piece):
        return jnp.concatenate(
            [
                jnp.where(
                    row_keys == line, parts[piece][step : step + 1, :], 0.0
                ).astype(jnp.bfloat16)
                for line, parts in zip(sensor_keys, split)
            ],
            axis=1,
        )

    def source_of(row_keys, sensor_keys, columns, step):
        total = None
        for piece in range(3):
            part = lax.dot_general(
                placed(row_keys, sensor_keys, step, piece),
                columns,
                NT,
                preferred_element_type=jnp.float32,
            )
            total = part if total is None else total + part
        return total

    last = steps - 1
    own_keys = keys(cells, 0.0)
    level_of = lax.broadcasted_iota(jnp.int32, (2 * layers, cols), 0)
    beside = (ny * grid_layers_rows)
    side_keys = row_key + jnp.where(
        level_of < layers,
        level_of * rows + (rows - 1 - beside),
        (level_of - layers) * rows + beside,
    ).astype(jnp.float32)
    wide_keys = jnp.concatenate(
        [
            own_keys,
            keys(rows, -float(rows)),
            keys(rows, float(cells)),
            side_keys,
            jnp.full((2 * layers, cols), -1.0, jnp.float32),
        ],
        axis=0,
    )
    wide = source_of(wide_keys, key_rows, in_column, last)
    far = float(tiles * grid_layers_rows * 4)
    moved_keys = [
        jnp.where(
            col_line == cols - 1.0,
            key_line + float(grid_layers_rows),
            jnp.where(col_line == 0.0, key_line - float(grid_layers_rows), -far),
        )
        for key_line, col_line in zip(key_rows, col_rows)
    ]
    at_edges = jnp.concatenate(
        [
            jnp.where(
                jnp.logical_or(
                    jnp.logical_and(col_ids == 0.0, line == cols - 1.0),
                    jnp.logical_and(col_ids == cols - 1.0, line == 0.0),
                ),
                1.0,
                0.0,
            ).astype(jnp.bfloat16)
            for line in col_rows
        ],
        axis=1,
    )
    edge = source_of(own_keys, moved_keys, at_edges, last)
    if steps > 1:
        sources[last - 1] = source_of(own_keys, key_rows, in_column, last - 1)

    field = adjoint + wide[:cells]
    low_src = wide[cells : cells + rows]
    high_src = wide[cells + rows : cells + 2 * rows]
    side_src = wide[cells + 2 * rows : cells + 2 * rows + 2 * layers]
    rows_low = first_x_in[0, layers : 2 * layers, :] * (
        first_x_in[0, 0:layers, :] + side_src[:layers]
    )
    rows_high = first_x_in[1, layers : 2 * layers, :] * (
        first_x_in[1, 0:layers, :] + side_src[layers:]
    )
    cols_adjoint = unpack_columns(packed, 0)
    cols_ratio = unpack_columns(packed, groups_of_rows)
    field = inner(field, ratio * field, own) + outer(
        spread_rows(rows_low, rows_high),
        cols_ratio * (cols_adjoint + edge),
        first_z_in[0, 2] * (first_z_in[0, 1] + low_src),
        first_z_in[1, 2] * (first_z_in[1, 1] + high_src),
    )
    field = refine(field)
    sens = ratio * field

    def one_step(turn, state):
        field, sens = state
        field = field + sources[last - turn]
        weighted = ratio * field
        copies = halo_copies(turn)
        at = turn - 1
        send_w[at] = weighted
        start(copies, (4, 5))
        left, right = pack_columns((weighted,))
        send_y[at, 0] = left
        send_y[at, 1] = right
        start(copies, (2, 3))
        send_x[at, 0, 0:layers, :] = pick_rows(weighted, 0)
        send_x[at, 1, 0:layers, :] = pick_rows(weighted, rows - 1)
        start(copies, (0, 1))
        field = inner(field, weighted, own)

        @pl.when(turn == 1)
        def _():
            for step in range(last - 2, -1, -1):
                sources[step] = source_of(own_keys, key_rows, in_column, step)

        arrive(copies)
        field = field + outer(
            spread_rows(recv_x[at, 0, 0:layers, :], recv_x[at, 1, 0:layers, :]),
            unpack_columns(recv_y[at, 0] + recv_y[at, 1], 0),
            recv_z[at, 0],
            recv_z[at, 1],
        )
        field = refine(field)
        return field, sens + ratio * field

    field, sens = lax.fori_loop(1, steps, one_step, (field, sens))
    adjoint_out[...] = field
    sens_out[...] = sens
    for offset in range(1, tiles):
        sensor_copy(offset).wait_send()
    sent(copies)

    @pl.loop(1, steps)
    def _(turn):
        sent(halo_copies(turn))


def solution(mesh):
    nx, ny, nz = mesh.shape["gx"], mesh.shape["gy"], mesh.shape["gz"]
    tiles = nx * ny

    def body(
        adjoint_final,
        conductivity,
        step_ratio,
        refine_rate,
        residual,
        sensor_tile,
        sensor_cell,
        substeps,
    ):
        layers, rows, cols = adjoint_final.shape
        steps, listed = residual.shape
        cells = layers * rows
        flat = (cells, cols)
        wide = -(-3 * layers // SUB) * SUB
        narrow = -(-layers // SUB) * SUB
        height = -(-(steps + 2) // SUB) * SUB
        turns = steps - 1
        f32 = jnp.float32
        vmem = pl.BlockSpec(memory_space=pltpu.VMEM)
        hbm = pl.BlockSpec(memory_space=pltpu.HBM)
        adjoint, sens = pl.pallas_call(
            functools.partial(kernel, (nx, ny, nz, layers, rows, cols, steps, listed)),
            out_shape=[jax.ShapeDtypeStruct(flat, f32)] * 2,
            in_specs=[hbm] * 8,
            out_specs=[vmem, vmem],
            scratch_shapes=[
                pltpu.VMEM((6, cells, cols), f32),
                pltpu.VMEM((steps, listed), f32),
                pltpu.VMEM((1, listed), jnp.int32),
                pltpu.VMEM((1, listed), jnp.int32),
                pltpu.SMEM(substeps.shape, jnp.int32),
                pltpu.VMEM((height, cols), f32),
                pltpu.VMEM((tiles, height, cols), f32),
                pltpu.VMEM((2, wide, cols), f32),
                pltpu.VMEM((2, wide, cols), f32),
                pltpu.VMEM((2, SUB, cols), f32),
                pltpu.VMEM((2, SUB, cols), f32),
                pltpu.VMEM((2, 3, rows, cols), f32),
                pltpu.VMEM((turns, cells, cols), f32),
                pltpu.VMEM((turns, 2, narrow, cols), f32),
                pltpu.VMEM((turns, 2, narrow, cols), f32),
                pltpu.VMEM((turns, 2, SUB, cols), f32),
                pltpu.VMEM((turns, 2, SUB, cols), f32),
                pltpu.VMEM((turns, 2, rows, cols), f32),
                pltpu.VMEM((steps, cells, cols), f32),
                pltpu.SemaphoreType.DMA((8,)),
                pltpu.SemaphoreType.DMA((tiles,)),
                pltpu.SemaphoreType.DMA((tiles,)),
                pltpu.SemaphoreType.DMA((steps, 6)),
                pltpu.SemaphoreType.DMA((steps, 6)),
            ],
            compiler_params=pltpu.CompilerParams(
                collective_id=0, has_side_effects=True, vmem_limit_bytes=63 * 1024 * 1024
            ),
        )(
            conductivity.reshape(3, *flat),
            adjoint_final.reshape(flat),
            step_ratio.reshape(flat),
            refine_rate.reshape(flat),
            residual,
            sensor_tile.reshape(1, listed),
            sensor_cell.reshape(1, listed),
            substeps,
        )
        return adjoint.reshape(layers, rows, cols), sens.reshape(layers, rows, cols)

    return jax.shard_map(
        body,
        mesh=mesh,
        in_specs=(
            P("gz", "gx", "gy"),
            P(None, "gz", "gx", "gy"),
            P("gz", "gx", "gy"),
            P("gz", "gx", "gy"),
            P(None, ("gx", "gy")),
            P(("gx", "gy")),
            P(("gx", "gy")),
            P(),
        ),
        out_specs=(P("gz", "gx", "gy"), P("gz", "gx", "gy")),
        check_vma=False,
    )
```

```python
import functools

import jax
import jax.numpy as jnp
from jax import lax
from jax.experimental import pallas as pl
from jax.experimental.pallas import tpu as pltpu
from jax.sharding import PartitionSpec as P

MESH = pl.DeviceIdType.MESH
MOST_TURNS = 6
SUB = 8
NT = (((1,), (1,)), ((), ()))


def harmonic(first, second):
    return 2.0 * first * second / (first + second)


def pieces_of(values):
    high = values.astype(jnp.bfloat16).astype(jnp.float32)
    rest = values - high
    middle = rest.astype(jnp.bfloat16).astype(jnp.float32)
    return high, middle, rest - middle


def kernel(
    sizes,
    cond_hbm,
    adjoint_hbm,
    ratio_hbm,
    rate_hbm,
    res_hbm,
    tile_hbm,
    cell_hbm,
    substeps_hbm,
    kept_out,
    moved_out,
    sens_out,
    base,
    res_in,
    tile_in,
    cell_in,
    substeps_ref,
    sensors,
    gathered,
    first_x,
    first_x_in,
    first_y,
    first_y_in,
    first_z_in,
    send_w,
    send_x,
    recv_x,
    send_y,
    recv_y,
    recv_z,
    results,
    load_sem,
    store_sem,
    sensor_send,
    sensor_recv,
    halo_send,
    halo_recv,
):
    nx, ny, nz, layers, rows, cols, steps, listed = sizes
    cells = layers * rows
    groups_of_rows = cells // SUB
    tiles = nx * ny
    x, y, z = lax.axis_index("gx"), lax.axis_index("gy"), lax.axis_index("gz")
    me = x * ny + y

    loads = [
        pltpu.make_async_copy(src, dst, load_sem.at[k])
        for k, (src, dst) in enumerate(
            (
                (res_hbm, res_in),
                (tile_hbm, tile_in),
                (cell_hbm, cell_in),
                (adjoint_hbm, base.at[3]),
                (ratio_hbm, base.at[4]),
                (cond_hbm, base.at[pl.ds(0, 3)]),
                (rate_hbm, base.at[5]),
                (substeps_hbm, substeps_ref),
            )
        )
    ]
    for load in loads:
        load.start()

    for ref in (first_x_in, first_y_in, first_z_in, recv_x, recv_y, recv_z, sensors):
        ref[...] = jnp.zeros_like(ref)

    sides = (
        (0, nx, x, -1),
        (0, nx, x, 1),
        (1, ny, y, -1),
        (1, ny, y, 1),
        (2, nz, z, -1),
        (2, nz, z, 1),
    )

    def device_at(axis, step):
        place = [x, y, z]
        place[axis] = place[axis] + step
        return tuple(place)

    def inside(count, place, step):
        return place > 0 if step < 0 else place < count - 1

    barrier = pltpu.get_barrier_semaphore()

    def sensor_peer(offset):
        there = lax.rem(me + offset, tiles)
        return (lax.div(there, ny), lax.rem(there, ny), z)

    for offset in range(1, tiles):
        pl.semaphore_signal(barrier, inc=1, device_id=sensor_peer(offset), device_id_type=MESH)
    for axis, count, place, step in sides[4:]:

        @pl.when(inside(count, place, step))
        def _():
            pl.semaphore_signal(
                barrier, inc=1, device_id=device_at(axis, step), device_id_type=MESH
            )

    for load in loads[:3]:
        load.wait()
    per = max(1, cols // listed)
    lane = lax.broadcasted_iota(jnp.int32, (1, cols), 1)
    cell = cell_in[...]
    grid_layers_rows = nz * cells
    key = tile_in[...] * grid_layers_rows + lax.div(cell, cols)
    column = lax.rem(cell, cols)
    for slot in range(per):
        here = pl.ds(slot * listed, listed)
        sensors[0:steps, here] = res_in[...]
        sensors[steps : steps + 1, here] = key.astype(jnp.float32)
        sensors[steps + 1 : steps + 2, here] = column.astype(jnp.float32)
    if per > 1:
        mine = lax.div(lane, listed) == lax.rem(me, per)
        sensors[...] = jnp.where(mine, sensors[...], 0.0)
    gathered[me] = sensors[...]

    neighbours = (
        (tiles - 1)
        + (z > 0).astype(jnp.int32)
        + (z < nz - 1).astype(jnp.int32)
    )
    pl.semaphore_wait(barrier, neighbours)

    def sensor_copy(offset):
        return pltpu.make_async_remote_copy(
            src_ref=sensors,
            dst_ref=gathered.at[me],
            send_sem=sensor_send.at[offset],
            recv_sem=sensor_recv.at[offset],
            device_id=sensor_peer(offset),
            device_id_type=MESH,
        )

    def sensor_arrival(offset):
        origin = lax.rem(me + (tiles - offset), tiles)
        return pltpu.make_async_remote_copy(
            src_ref=sensors,
            dst_ref=gathered.at[origin],
            send_sem=sensor_send.at[offset],
            recv_sem=sensor_recv.at[offset],
            device_id=sensor_peer(offset),
            device_id_type=MESH,
        )

    for offset in range(1, tiles):
        sensor_copy(offset).start()

    for load in loads[3:]:
        load.wait()
    lanes = lax.broadcasted_iota(jnp.int32, (SUB, cols), 1)

    def pack_columns(arrays):
        to_left = jnp.zeros((SUB, cols), jnp.float32)
        to_right = jnp.zeros((SUB, cols), jnp.float32)
        spot = 0
        for array in arrays:
            for part in range(groups_of_rows):
                block = array[part * SUB : (part + 1) * SUB, :]
                left = pltpu.roll(block, spot % cols, 1)
                right = pltpu.roll(block, (spot + 2) % cols, 1)
                to_left = jnp.where(lanes == spot, left, to_left)
                to_right = jnp.where(lanes == spot + 1, right, to_right)
                spot += 2
        return to_left, to_right

    def unpack_columns(packed, spot):
        return jnp.concatenate(
            [
                pltpu.roll(packed, (cols - 2 * (spot + part) - 1) % cols, 1)
                for part in range(groups_of_rows)
            ],
            axis=0,
        )

    def pick_rows(array, row):
        return jnp.concatenate(
            [array[level * rows + row : level * rows + row + 1, :] for level in range(layers)],
            axis=0,
        )

    def spread_rows(low, high):
        half = rows // 2
        parts = []
        for level in range(layers):
            parts.append(jnp.broadcast_to(low[level : level + 1, :], (half, cols)))
            parts.append(jnp.broadcast_to(high[level : level + 1, :], (rows - half, cols)))
        return jnp.concatenate(parts, axis=0)

    c0, c1, c2 = base[0], base[1], base[2]
    adjoint, ratio, rate = base[3], base[4], base[5]

    def halo_copies(turn):
        copies = []
        for side, (axis, count, place, step) in enumerate(sides):
            way = side % 2
            if turn == 0:
                source, target = (
                    (first_x.at[way], first_x_in.at[1 - way]),
                    (first_y.at[way], first_y_in.at[1 - way]),
                    (
                        base.at[pl.ds(2, 3), pl.ds(way * (cells - rows), rows)],
                        first_z_in.at[1 - way],
                    ),
                )[axis]
            else:
                at = turn - 1
                source, target = (
                    (send_x.at[at, way], recv_x.at[at, 1 - way]),
                    (send_y.at[at, way], recv_y.at[at, 1 - way]),
                    (
                        send_w.at[at, pl.ds(way * (cells - rows), rows)],
                        recv_z.at[at, 1 - way],
                    ),
                )[axis]
            copy = pltpu.make_async_remote_copy(
                src_ref=source,
                dst_ref=target,
                send_sem=halo_send.at[turn, side],
                recv_sem=halo_recv.at[turn, 2 * axis + 1 - way],
                device_id=device_at(axis, step),
                device_id_type=MESH,
            )
            arrival = pltpu.make_async_remote_copy(
                src_ref=source,
                dst_ref=(
                    (first_x_in, first_y_in, first_z_in)[axis].at[way]
                    if turn == 0
                    else (recv_x, recv_y, recv_z)[axis].at[turn - 1, way]
                ),
                send_sem=halo_send.at[turn, side],
                recv_sem=halo_recv.at[turn, side],
                device_id=device_at(axis, step),
                device_id_type=MESH,
            )
            copies.append((inside(count, place, step), copy, arrival))
        return copies

    def start(copies, chosen):
        for side in chosen:
            valid, copy, _ = copies[side]
            pl.when(valid)(copy.start)

    def arrive(copies):
        for valid, _, arrival in copies:
            pl.when(valid)(arrival.wait_recv)

    def sent(copies):
        for valid, copy, _ in copies:
            pl.when(valid)(copy.wait_send)

    copies = halo_copies(0)
    start(copies, (4, 5))
    for k, array in enumerate((adjoint, ratio, c0)):
        first_x[0, k * layers : (k + 1) * layers, :] = pick_rows(array, 0)
        first_x[1, k * layers : (k + 1) * layers, :] = pick_rows(array, rows - 1)
    left, right = pack_columns((adjoint, ratio, c1))
    first_y[0] = left
    first_y[1] = right

    start(copies, (2, 3, 0, 1))

    full = (cells, cols)
    row_in = lax.rem(lax.broadcasted_iota(jnp.int32, full, 0), rows)
    col_in = lax.broadcasted_iota(jnp.int32, full, 1)
    top, bottom = row_in == 0, row_in == rows - 1
    first_col, last_col = col_in == 0, col_in == cols - 1

    def next_row(array):
        return pltpu.roll(array, cells - 1, 0)

    def prev_row(array):
        return pltpu.roll(array, 1, 0)

    def next_col(array):
        return pltpu.roll(array, cols - 1, 1)

    def prev_col(array):
        return pltpu.roll(array, 1, 1)

    row_next = jnp.where(bottom, 0.0, harmonic(c0, next_row(c0)))
    row_prev = prev_row(row_next)
    col_next = jnp.where(last_col, 0.0, harmonic(c1, next_col(c1)))
    col_prev = prev_col(col_next)
    between = harmonic(c2[: cells - rows], c2[rows:])
    no_layer = jnp.zeros((rows, cols), jnp.float32)
    rate_next_row = jnp.where(bottom, 0.0, next_row(rate))
    rate_prev_row = jnp.where(top, 0.0, prev_row(rate))
    rate_next_col = jnp.where(last_col, 0.0, next_col(rate))
    rate_prev_col = jnp.where(first_col, 0.0, prev_col(rate))
    around = (
        4.0
        - top.astype(jnp.float32)
        - bottom.astype(jnp.float32)
        - first_col.astype(jnp.float32)
        - last_col.astype(jnp.float32)
    )
    stay = 1.0 - around * rate
    turns = jnp.full(full, substeps_ref[x, y])
    inner_faces = (
        row_next
        + row_prev
        + col_next
        + col_prev
        + jnp.concatenate([between, no_layer], axis=0)
        + jnp.concatenate([no_layer, between], axis=0)
    )

    def halves(field):
        around_it = (rate_next_row * next_row(field) + rate_prev_row * prev_row(field)) + (
            rate_next_col * next_col(field) + rate_prev_col * prev_col(field)
        )
        return stay * field, around_it

    def refine(field, count):
        for turn in range(count):
            kept, moved = halves(field)
            field = jnp.where(turns > turn, kept + moved, field)
        return field

    def inner(field, weighted, own):
        return (
            own * field
            + (row_next * next_row(weighted) + row_prev * prev_row(weighted))
            + (col_next * next_col(weighted) + col_prev * prev_col(weighted))
            + jnp.concatenate([between * weighted[rows:], no_layer], axis=0)
            + jnp.concatenate([no_layer, between * weighted[: cells - rows]], axis=0)
        )

    row_key = (me * grid_layers_rows + z * cells).astype(jnp.float32)

    def keys(count, start_at):
        place = lax.broadcasted_iota(jnp.int32, (count, cols), 0).astype(jnp.float32)
        return place + (row_key + start_at)

    for offset in range(1, tiles):
        sensor_arrival(offset).wait_recv()
    blocks = []
    folded = max(1, tiles // per)
    for block in range(folded):
        total = gathered[block * per]
        for slot in range(1, per):
            total = total + gathered[block * per + slot]
        blocks.append(total)
    key_rows = [total[steps : steps + 1, :] for total in blocks]
    col_rows = [total[steps + 1 : steps + 2, :] for total in blocks]
    split = [pieces_of(total[0:steps, :]) for total in blocks]
    col_ids = lax.broadcasted_iota(jnp.int32, (cols, cols), 0).astype(jnp.float32)
    in_column = jnp.concatenate(
        [jnp.where(col_ids == line, 1.0, 0.0).astype(jnp.bfloat16) for line in col_rows], axis=1
    )

    def placed(row_keys, sensor_keys, step, piece):
        return jnp.concatenate(
            [
                jnp.where(
                    row_keys == line, parts[piece][step : step + 1, :], 0.0
                ).astype(jnp.bfloat16)
                for line, parts in zip(sensor_keys, split)
            ],
            axis=1,
        )

    def source_of(row_keys, sensor_keys, columns, step):
        total = None
        for piece in range(3):
            part = lax.dot_general(
                placed(row_keys, sensor_keys, step, piece),
                columns,
                NT,
                preferred_element_type=jnp.float32,
            )
            total = part if total is None else total + part
        return total

    last = steps - 1
    own_keys = keys(cells, 0.0)
    level_of = lax.broadcasted_iota(jnp.int32, (2 * layers, cols), 0)
    beside = (ny * grid_layers_rows)
    side_keys = row_key + jnp.where(
        level_of < layers,
        level_of * rows + (rows - 1 - beside),
        (level_of - layers) * rows + beside,
    ).astype(jnp.float32)
    wide_keys = jnp.concatenate(
        [
            own_keys,
            keys(rows, -float(rows)),
            keys(rows, float(cells)),
            side_keys,
            jnp.full((2 * layers, cols), -1.0, jnp.float32),
        ],
        axis=0,
    )
    wide = source_of(wide_keys, key_rows, in_column, last)
    far = float(tiles * grid_layers_rows * 4)
    moved_keys = [
        jnp.where(
            col_line == cols - 1.0,
            key_line + float(grid_layers_rows),
            jnp.where(col_line == 0.0, key_line - float(grid_layers_rows), -far),
        )
        for key_line, col_line in zip(key_rows, col_rows)
    ]
    at_edges = jnp.concatenate(
        [
            jnp.where(col_ids == (cols - 1.0) - line, 1.0, 0.0).astype(jnp.bfloat16)
            for line in col_rows
        ],
        axis=1,
    )
    edge = source_of(own_keys, moved_keys, at_edges, last)

    arrive(copies)

    row_halo = spread_rows(
        first_x_in[0, 2 * layers : 3 * layers, :], first_x_in[1, 2 * layers : 3 * layers, :]
    )
    row_face = jnp.where(jnp.logical_or(top, bottom), harmonic(c0, row_halo), 0.0)
    packed = first_y_in[0] + first_y_in[1]
    col_halo = unpack_columns(packed, 2 * groups_of_rows)
    col_face = jnp.where(jnp.logical_or(first_col, last_col), harmonic(c1, col_halo), 0.0)
    low_face = harmonic(c2[:rows], first_z_in[0, 0])
    high_face = harmonic(c2[cells - rows :], first_z_in[1, 0])
    middle = cells - 2 * rows

    def with_ends(low, high):
        parts = [low]
        if middle > 0:
            parts.append(jnp.zeros((middle, cols), jnp.float32))
        return jnp.concatenate(parts + [high], axis=0)

    all_faces = inner_faces + row_face + col_face + with_ends(low_face, high_face)
    own = 1.0 - ratio * all_faces

    def outer(row_values, col_values, low_values, high_values):
        return (
            row_face * row_values
            + col_face * col_values
            + with_ends(low_face * low_values, high_face * high_values)
        )

    field = adjoint + wide[:cells]
    low_src = wide[cells : cells + rows]
    high_src = wide[cells + rows : cells + 2 * rows]
    side_src = wide[cells + 2 * rows : cells + 2 * rows + 2 * layers]
    rows_low = first_x_in[0, layers : 2 * layers, :] * (
        first_x_in[0, 0:layers, :] + side_src[:layers]
    )
    rows_high = first_x_in[1, layers : 2 * layers, :] * (
        first_x_in[1, 0:layers, :] + side_src[layers:]
    )
    cols_adjoint = unpack_columns(packed, 0)
    cols_ratio = unpack_columns(packed, groups_of_rows)
    field = inner(field, ratio * field, own) + outer(
        spread_rows(rows_low, rows_high),
        cols_ratio * (cols_adjoint + edge),
        first_z_in[0, 2] * (first_z_in[0, 1] + low_src),
        first_z_in[1, 2] * (first_z_in[1, 1] + high_src),
    )
    next_source = source_of(own_keys, key_rows, in_column, last - 1)
    field = refine(field, MOST_TURNS)
    sens = ratio * field

    pending = [copies]
    sources = {last - 1: next_source}
    for turn in range(1, steps):
        step = last - turn
        field = field + sources[step]
        weighted = ratio * field
        copies = halo_copies(turn)
        at = turn - 1
        send_w[at] = weighted
        start(copies, (4, 5))
        left, right = pack_columns((weighted,))
        send_y[at, 0] = left
        send_y[at, 1] = right
        start(copies, (2, 3))
        send_x[at, 0, 0:layers, :] = pick_rows(weighted, 0)
        send_x[at, 1, 0:layers, :] = pick_rows(weighted, rows - 1)
        start(copies, (0, 1))
        pending.append(copies)
        field = inner(field, weighted, own)
        if step > 0:
            sources[step - 1] = source_of(own_keys, key_rows, in_column, step - 1)
        arrive(copies)
        field = field + outer(
            spread_rows(recv_x[at, 0, 0:layers, :], recv_x[at, 1, 0:layers, :]),
            unpack_columns(recv_y[at, 0] + recv_y[at, 1], 0),
            recv_z[at, 0],
            recv_z[at, 1],
        )
        if step > 0:
            field = refine(field, MOST_TURNS)
            sens = sens + ratio * field

    field = refine(field, MOST_TURNS - 1)
    kept, moved = halves(field)
    active = turns > MOST_TURNS - 1
    results[0] = jnp.where(active, kept, field)
    results[1] = jnp.where(active, moved, 0.0)
    results[2] = sens
    stores = [
        pltpu.make_async_copy(results.at[k], out, store_sem.at[k])
        for k, out in enumerate((kept_out, moved_out, sens_out))
    ]
    for store in stores:
        store.start()
    for offset in range(1, tiles):
        sensor_copy(offset).wait_send()
    for copies in pending:
        sent(copies)
    for store in stores:
        store.wait()


def solution(mesh):
    nx, ny, nz = mesh.shape["gx"], mesh.shape["gy"], mesh.shape["gz"]
    tiles = nx * ny

    def body(
        adjoint_final,
        conductivity,
        step_ratio,
        refine_rate,
        residual,
        sensor_tile,
        sensor_cell,
        substeps,
    ):
        layers, rows, cols = adjoint_final.shape
        steps, listed = residual.shape
        cells = layers * rows
        flat = (cells, cols)
        wide = -(-3 * layers // SUB) * SUB
        narrow = -(-layers // SUB) * SUB
        height = -(-(steps + 2) // SUB) * SUB
        turns = steps - 1
        f32 = jnp.float32
        hbm = pl.BlockSpec(memory_space=pltpu.HBM)
        kept, moved, sens = pl.pallas_call(
            functools.partial(kernel, (nx, ny, nz, layers, rows, cols, steps, listed)),
            out_shape=[jax.ShapeDtypeStruct(flat, f32)] * 3,
            in_specs=[hbm] * 8,
            out_specs=[hbm] * 3,
            scratch_shapes=[
                pltpu.VMEM((6, cells, cols), f32),
                pltpu.VMEM((steps, listed), f32),
                pltpu.VMEM((1, listed), jnp.int32),
                pltpu.VMEM((1, listed), jnp.int32),
                pltpu.SMEM(substeps.shape, jnp.int32),
                pltpu.VMEM((height, cols), f32),
                pltpu.VMEM((tiles, height, cols), f32),
                pltpu.VMEM((2, wide, cols), f32),
                pltpu.VMEM((2, wide, cols), f32),
                pltpu.VMEM((2, SUB, cols), f32),
                pltpu.VMEM((2, SUB, cols), f32),
                pltpu.VMEM((2, 3, rows, cols), f32),
                pltpu.VMEM((turns, cells, cols), f32),
                pltpu.VMEM((turns, 2, narrow, cols), f32),
                pltpu.VMEM((turns, 2, narrow, cols), f32),
                pltpu.VMEM((turns, 2, SUB, cols), f32),
                pltpu.VMEM((turns, 2, SUB, cols), f32),
                pltpu.VMEM((turns, 2, rows, cols), f32),
                pltpu.VMEM((3, cells, cols), f32),
                pltpu.SemaphoreType.DMA((8,)),
                pltpu.SemaphoreType.DMA((3,)),
                pltpu.SemaphoreType.DMA((tiles,)),
                pltpu.SemaphoreType.DMA((tiles,)),
                pltpu.SemaphoreType.DMA((steps, 6)),
                pltpu.SemaphoreType.DMA((steps, 6)),
            ],
            compiler_params=pltpu.CompilerParams(
                collective_id=0, has_side_effects=True, vmem_limit_bytes=63 * 1024 * 1024
            ),
        )(
            conductivity.reshape(3, *flat),
            adjoint_final.reshape(flat),
            step_ratio.reshape(flat),
            refine_rate.reshape(flat),
            residual,
            sensor_tile.reshape(1, listed),
            sensor_cell.reshape(1, listed),
            substeps,
        )
        shape = adjoint_final.shape
        adjoint = kept.reshape(shape) + moved.reshape(shape)
        return adjoint, sens.reshape(shape) + step_ratio * adjoint

    return jax.shard_map(
        body,
        mesh=mesh,
        in_specs=(
            P("gz", "gx", "gy"),
            P(None, "gz", "gx", "gy"),
            P("gz", "gx", "gy"),
            P("gz", "gx", "gy"),
            P(None, ("gx", "gy")),
            P(("gx", "gy")),
            P(("gx", "gy")),
            P(),
        ),
        out_specs=(P("gz", "gx", "gy"), P("gz", "gx", "gy")),
        check_vma=False,
    )
```

```python
import functools

import jax
import jax.numpy as jnp
from jax import lax
from jax.experimental import pallas as pl
from jax.experimental.pallas import tpu as pltpu
from jax.sharding import PartitionSpec as P

MESH = pl.DeviceIdType.MESH
MOST_TURNS = 6
SUB = 8
NT = (((1,), (1,)), ((), ()))


def harmonic(first, second):
    return 2.0 * first * second / (first + second)


def pieces_of(values):
    high = values.astype(jnp.bfloat16).astype(jnp.float32)
    rest = values - high
    middle = rest.astype(jnp.bfloat16).astype(jnp.float32)
    return high, middle, rest - middle


def kernel(
    sizes,
    cond_hbm,
    adjoint_hbm,
    ratio_hbm,
    rate_hbm,
    res_hbm,
    tile_hbm,
    cell_hbm,
    substeps_hbm,
    kept_out,
    moved_out,
    sens_out,
    base,
    res_in,
    tile_in,
    cell_in,
    substeps_ref,
    sensors,
    gathered,
    first_x,
    first_x_in,
    first_y,
    first_y_in,
    first_z_in,
    send_w,
    send_x,
    recv_x,
    send_y,
    recv_y,
    recv_z,
    results,
    shifted,
    load_sem,
    store_sem,
    sensor_send,
    sensor_recv,
    halo_send,
    halo_recv,
):
    nx, ny, nz, layers, rows, cols, steps, listed = sizes
    cells = layers * rows
    groups_of_rows = cells // SUB
    tiles = nx * ny
    x, y, z = lax.axis_index("gx"), lax.axis_index("gy"), lax.axis_index("gz")
    me = x * ny + y

    loads = [
        pltpu.make_async_copy(src, dst, load_sem.at[k])
        for k, (src, dst) in enumerate(
            (
                (res_hbm, res_in),
                (tile_hbm, tile_in),
                (cell_hbm, cell_in),
                (adjoint_hbm, base.at[3]),
                (ratio_hbm, base.at[4]),
                (cond_hbm, base.at[pl.ds(0, 3)]),
                (rate_hbm, base.at[5]),
                (substeps_hbm, substeps_ref),
            )
        )
    ]
    for load in loads:
        load.start()

    for ref in (first_x_in, first_y_in, first_z_in, recv_x, recv_y, recv_z, sensors, shifted):
        ref[...] = jnp.zeros_like(ref)

    sides = (
        (0, nx, x, -1),
        (0, nx, x, 1),
        (1, ny, y, -1),
        (1, ny, y, 1),
        (2, nz, z, -1),
        (2, nz, z, 1),
    )

    def device_at(axis, step):
        place = [x, y, z]
        place[axis] = place[axis] + step
        return tuple(place)

    def inside(count, place, step):
        return place > 0 if step < 0 else place < count - 1

    barrier = pltpu.get_barrier_semaphore()

    def sensor_peer(offset):
        there = lax.rem(me + offset, tiles)
        return (lax.div(there, ny), lax.rem(there, ny), z)

    for offset in range(1, tiles):
        pl.semaphore_signal(barrier, inc=1, device_id=sensor_peer(offset), device_id_type=MESH)
    for axis, count, place, step in sides[4:]:

        @pl.when(inside(count, place, step))
        def _():
            pl.semaphore_signal(
                barrier, inc=1, device_id=device_at(axis, step), device_id_type=MESH
            )

    for load in loads[:3]:
        load.wait()
    per = max(1, cols // listed)
    lane = lax.broadcasted_iota(jnp.int32, (1, cols), 1)
    cell = cell_in[...]
    grid_layers_rows = nz * cells
    key = tile_in[...] * grid_layers_rows + lax.div(cell, cols)
    column = lax.rem(cell, cols)
    for slot in range(per):
        here = pl.ds(slot * listed, listed)
        sensors[0:steps, here] = res_in[...]
        sensors[steps : steps + 1, here] = key.astype(jnp.float32)
        sensors[steps + 1 : steps + 2, here] = column.astype(jnp.float32)
    if per > 1:
        mine = lax.div(lane, listed) == lax.rem(me, per)
        sensors[...] = jnp.where(mine, sensors[...], 0.0)
    gathered[me] = sensors[...]

    neighbours = (
        (tiles - 1)
        + (z > 0).astype(jnp.int32)
        + (z < nz - 1).astype(jnp.int32)
    )
    pl.semaphore_wait(barrier, neighbours)

    def sensor_copy(offset):
        return pltpu.make_async_remote_copy(
            src_ref=sensors,
            dst_ref=gathered.at[me],
            send_sem=sensor_send.at[offset],
            recv_sem=sensor_recv.at[offset],
            device_id=sensor_peer(offset),
            device_id_type=MESH,
        )

    def sensor_arrival(offset):
        origin = lax.rem(me + (tiles - offset), tiles)
        return pltpu.make_async_remote_copy(
            src_ref=sensors,
            dst_ref=gathered.at[origin],
            send_sem=sensor_send.at[offset],
            recv_sem=sensor_recv.at[offset],
            device_id=sensor_peer(offset),
            device_id_type=MESH,
        )

    for offset in range(1, tiles):
        sensor_copy(offset).start()

    for load in loads[3:]:
        load.wait()
    lanes = lax.broadcasted_iota(jnp.int32, (SUB, cols), 1)

    def pack_columns(arrays):
        to_left = jnp.zeros((SUB, cols), jnp.float32)
        to_right = jnp.zeros((SUB, cols), jnp.float32)
        spot = 0
        for array in arrays:
            for part in range(groups_of_rows):
                block = array[part * SUB : (part + 1) * SUB, :]
                left = pltpu.roll(block, spot % cols, 1)
                right = pltpu.roll(block, (spot + 2) % cols, 1)
                to_left = jnp.where(lanes == spot, left, to_left)
                to_right = jnp.where(lanes == spot + 1, right, to_right)
                spot += 2
        return to_left, to_right

    def unpack_columns(packed, spot):
        return jnp.concatenate(
            [
                pltpu.roll(packed, (cols - 2 * (spot + part) - 1) % cols, 1)
                for part in range(groups_of_rows)
            ],
            axis=0,
        )

    def pick_rows(array, row):
        return jnp.concatenate(
            [array[level * rows + row : level * rows + row + 1, :] for level in range(layers)],
            axis=0,
        )

    def spread_rows(low, high):
        half = rows // 2
        parts = []
        for level in range(layers):
            parts.append(jnp.broadcast_to(low[level : level + 1, :], (half, cols)))
            parts.append(jnp.broadcast_to(high[level : level + 1, :], (rows - half, cols)))
        return jnp.concatenate(parts, axis=0)

    c0, c1, c2 = base[0], base[1], base[2]
    adjoint, ratio, rate = base[3], base[4], base[5]

    def halo_copies(turn):
        copies = []
        for side, (axis, count, place, step) in enumerate(sides):
            way = side % 2
            if turn == 0:
                source, target = (
                    (first_x.at[way], first_x_in.at[1 - way]),
                    (first_y.at[way], first_y_in.at[1 - way]),
                    (
                        base.at[pl.ds(2, 3), pl.ds(way * (cells - rows), rows)],
                        first_z_in.at[1 - way],
                    ),
                )[axis]
            else:
                at = turn - 1
                source, target = (
                    (send_x.at[at, way], recv_x.at[at, 1 - way]),
                    (send_y.at[at, way], recv_y.at[at, 1 - way]),
                    (
                        send_w.at[at, pl.ds(way * (cells - rows), rows)],
                        recv_z.at[at, 1 - way],
                    ),
                )[axis]
            copy = pltpu.make_async_remote_copy(
                src_ref=source,
                dst_ref=target,
                send_sem=halo_send.at[turn, side],
                recv_sem=halo_recv.at[turn, 2 * axis + 1 - way],
                device_id=device_at(axis, step),
                device_id_type=MESH,
            )
            arrival = pltpu.make_async_remote_copy(
                src_ref=source,
                dst_ref=(
                    (first_x_in, first_y_in, first_z_in)[axis].at[way]
                    if turn == 0
                    else (recv_x, recv_y, recv_z)[axis].at[turn - 1, way]
                ),
                send_sem=halo_send.at[turn, side],
                recv_sem=halo_recv.at[turn, side],
                device_id=device_at(axis, step),
                device_id_type=MESH,
            )
            copies.append((inside(count, place, step), copy, arrival))
        return copies

    def start(copies, chosen):
        for side in chosen:
            valid, copy, _ = copies[side]
            pl.when(valid)(copy.start)

    def arrive(copies, chosen):
        for side in chosen:
            valid, _, arrival = copies[side]
            pl.when(valid)(arrival.wait_recv)

    def sent(copies):
        for valid, copy, _ in copies:
            pl.when(valid)(copy.wait_send)

    copies = halo_copies(0)
    start(copies, (4, 5))
    for k, array in enumerate((adjoint, ratio, c0)):
        first_x[0, k * layers : (k + 1) * layers, :] = pick_rows(array, 0)
        first_x[1, k * layers : (k + 1) * layers, :] = pick_rows(array, rows - 1)
    left, right = pack_columns((adjoint, ratio, c1))
    first_y[0] = left
    first_y[1] = right

    start(copies, (2, 3, 0, 1))

    full = (cells, cols)
    row_in = lax.rem(lax.broadcasted_iota(jnp.int32, full, 0), rows)
    col_in = lax.broadcasted_iota(jnp.int32, full, 1)
    top, bottom = row_in == 0, row_in == rows - 1
    first_col, last_col = col_in == 0, col_in == cols - 1

    def next_row(array):
        return pltpu.roll(array, cells - 1, 0)

    def prev_row(array):
        return pltpu.roll(array, 1, 0)

    def next_col(array):
        return pltpu.roll(array, cols - 1, 1)

    def prev_col(array):
        return pltpu.roll(array, 1, 1)

    row_next = jnp.where(bottom, 0.0, harmonic(c0, next_row(c0)))
    row_prev = prev_row(row_next)
    col_next = jnp.where(last_col, 0.0, harmonic(c1, next_col(c1)))
    col_prev = prev_col(col_next)
    between = harmonic(c2[: cells - rows], c2[rows:])
    no_layer = jnp.zeros((rows, cols), jnp.float32)
    rate_next_row = jnp.where(bottom, 0.0, next_row(rate))
    rate_prev_row = jnp.where(top, 0.0, prev_row(rate))
    rate_next_col = jnp.where(last_col, 0.0, next_col(rate))
    rate_prev_col = jnp.where(first_col, 0.0, prev_col(rate))
    around = (
        4.0
        - top.astype(jnp.float32)
        - bottom.astype(jnp.float32)
        - first_col.astype(jnp.float32)
        - last_col.astype(jnp.float32)
    )
    stay = 1.0 - around * rate
    turns = jnp.full(full, substeps_ref[x, y])
    inner_faces = (
        row_next
        + row_prev
        + col_next
        + col_prev
        + jnp.concatenate([between, no_layer], axis=0)
        + jnp.concatenate([no_layer, between], axis=0)
    )

    def halves(field, turn):
        half = turn % 2
        shifted[half, SUB : SUB + cells, :] = field
        below = shifted[half, SUB + 1 : SUB + 1 + cells, :]
        above = shifted[half, SUB - 1 : SUB - 1 + cells, :]
        around_it = (rate_next_row * below + rate_prev_row * above) + (
            rate_next_col * next_col(field) + rate_prev_col * prev_col(field)
        )
        return stay * field, around_it

    def refine(field, count):
        for turn in range(count):
            kept, moved = halves(field, turn)
            field = jnp.where(turns > turn, kept + moved, field)
        return field

    def inner(field, weighted, own):
        return (
            own * field
            + (row_next * next_row(weighted) + row_prev * prev_row(weighted))
            + (col_next * next_col(weighted) + col_prev * prev_col(weighted))
            + jnp.concatenate([between * weighted[rows:], no_layer], axis=0)
            + jnp.concatenate([no_layer, between * weighted[: cells - rows]], axis=0)
        )

    row_key = (me * grid_layers_rows + z * cells).astype(jnp.float32)

    def keys(count, start_at):
        place = lax.broadcasted_iota(jnp.int32, (count, cols), 0).astype(jnp.float32)
        return place + (row_key + start_at)

    for offset in range(1, tiles):
        sensor_arrival(offset).wait_recv()
    blocks = []
    folded = max(1, tiles // per)
    for block in range(folded):
        total = gathered[block * per]
        for slot in range(1, per):
            total = total + gathered[block * per + slot]
        blocks.append(total)
    key_rows = [total[steps : steps + 1, :] for total in blocks]
    col_rows = [total[steps + 1 : steps + 2, :] for total in blocks]
    split = [pieces_of(total[0:steps, :]) for total in blocks]
    col_ids = lax.broadcasted_iota(jnp.int32, (cols, cols), 0).astype(jnp.float32)
    in_column = jnp.concatenate(
        [jnp.where(col_ids == line, 1.0, 0.0).astype(jnp.bfloat16) for line in col_rows], axis=1
    )

    def placed(row_keys, sensor_keys, step, piece):
        return jnp.concatenate(
            [
                jnp.where(
                    row_keys == line, parts[piece][step : step + 1, :], 0.0
                ).astype(jnp.bfloat16)
                for line, parts in zip(sensor_keys, split)
            ],
            axis=1,
        )

    def source_of(row_keys, sensor_keys, columns, step):
        total = None
        for piece in range(3):
            part = lax.dot_general(
                placed(row_keys, sensor_keys, step, piece),
                columns,
                NT,
                preferred_element_type=jnp.float32,
            )
            total = part if total is None else total + part
        return total

    last = steps - 1
    own_keys = keys(cells, 0.0)
    level_of = lax.broadcasted_iota(jnp.int32, (2 * layers, cols), 0)
    beside = (ny * grid_layers_rows)
    side_keys = row_key + jnp.where(
        level_of < layers,
        level_of * rows + (rows - 1 - beside),
        (level_of - layers) * rows + beside,
    ).astype(jnp.float32)
    wide_keys = jnp.concatenate(
        [
            own_keys,
            keys(rows, -float(rows)),
            keys(rows, float(cells)),
            side_keys,
            jnp.full((2 * layers, cols), -1.0, jnp.float32),
        ],
        axis=0,
    )
    wide = source_of(wide_keys, key_rows, in_column, last)
    far = float(tiles * grid_layers_rows * 4)
    moved_keys = [
        jnp.where(
            col_line == cols - 1.0,
            key_line + float(grid_layers_rows),
            jnp.where(col_line == 0.0, key_line - float(grid_layers_rows), -far),
        )
        for key_line, col_line in zip(key_rows, col_rows)
    ]
    at_edges = jnp.concatenate(
        [
            jnp.where(col_ids == (cols - 1.0) - line, 1.0, 0.0).astype(jnp.bfloat16)
            for line in col_rows
        ],
        axis=1,
    )
    edge = source_of(own_keys, moved_keys, at_edges, last)

    arrive(copies, (0, 1, 4, 5))
    row_halo = spread_rows(
        first_x_in[0, 2 * layers : 3 * layers, :], first_x_in[1, 2 * layers : 3 * layers, :]
    )
    row_face = jnp.where(jnp.logical_or(top, bottom), harmonic(c0, row_halo), 0.0)
    low_face = harmonic(c2[:rows], first_z_in[0, 0])
    high_face = harmonic(c2[cells - rows :], first_z_in[1, 0])
    middle = cells - 2 * rows

    def with_ends(low, high):
        parts = [low]
        if middle > 0:
            parts.append(jnp.zeros((middle, cols), jnp.float32))
        return jnp.concatenate(parts + [high], axis=0)

    near_faces = inner_faces + row_face + with_ends(low_face, high_face)
    row_values = spread_rows(
        first_x_in[0, layers : 2 * layers, :]
        * (first_x_in[0, 0:layers, :] + wide[cells + 2 * rows : cells + 2 * rows + layers]),
        first_x_in[1, layers : 2 * layers, :]
        * (
            first_x_in[1, 0:layers, :]
            + wide[cells + 2 * rows + layers : cells + 2 * rows + 2 * layers]
        ),
    )
    low_values = first_z_in[0, 2] * (first_z_in[0, 1] + wide[cells : cells + rows])
    high_values = first_z_in[1, 2] * (first_z_in[1, 1] + wide[cells + rows : cells + 2 * rows])

    def outer(row_values, low_values, high_values):
        return row_face * row_values + with_ends(
            low_face * low_values, high_face * high_values
        )

    arrive(copies, (2, 3))
    packed = first_y_in[0] + first_y_in[1]
    col_halo = unpack_columns(packed, 2 * groups_of_rows)
    col_face = jnp.where(jnp.logical_or(first_col, last_col), harmonic(c1, col_halo), 0.0)
    own = 1.0 - ratio * (near_faces + col_face)

    field = adjoint + wide[:cells]
    cols_adjoint = unpack_columns(packed, 0)
    cols_ratio = unpack_columns(packed, groups_of_rows)
    field = (
        inner(field, ratio * field, own)
        + outer(row_values, low_values, high_values)
        + col_face * (cols_ratio * (cols_adjoint + edge))
    )
    next_source = source_of(own_keys, key_rows, in_column, last - 1)
    field = refine(field, MOST_TURNS)
    sens = ratio * field

    stores = [
        pltpu.make_async_copy(results.at[k], out, store_sem.at[k])
        for k, out in enumerate((kept_out, moved_out, sens_out))
    ]
    pending = [copies]
    sources = {last - 1: next_source}
    for turn in range(1, steps):
        step = last - turn
        field = field + sources[step]
        weighted = ratio * field
        copies = halo_copies(turn)
        at = turn - 1
        send_w[at] = weighted
        start(copies, (4, 5))
        left, right = pack_columns((weighted,))
        send_y[at, 0] = left
        send_y[at, 1] = right
        start(copies, (2, 3))
        send_x[at, 0, 0:layers, :] = pick_rows(weighted, 0)
        send_x[at, 1, 0:layers, :] = pick_rows(weighted, rows - 1)
        start(copies, (0, 1))
        pending.append(copies)
        if step == 0:
            results[2] = sens
            stores[2].start()
        field = inner(field, weighted, own)
        if step > 0:
            sources[step - 1] = source_of(own_keys, key_rows, in_column, step - 1)
        arrive(copies, (0, 1, 4, 5))
        field = field + outer(
            spread_rows(recv_x[at, 0, 0:layers, :], recv_x[at, 1, 0:layers, :]),
            recv_z[at, 0],
            recv_z[at, 1],
        )
        arrive(copies, (2, 3))
        field = field + col_face * unpack_columns(recv_y[at, 0] + recv_y[at, 1], 0)
        if step > 0:
            field = refine(field, MOST_TURNS)
            sens = sens + ratio * field

    field = refine(field, MOST_TURNS - 1)
    kept, moved = halves(field, MOST_TURNS - 1)
    active = turns > MOST_TURNS - 1
    results[0] = jnp.where(active, kept, field)
    results[1] = jnp.where(active, moved, 0.0)
    for store in stores[:2]:
        store.start()
    for offset in range(1, tiles):
        sensor_copy(offset).wait_send()
    for copies in pending:
        sent(copies)
    for store in stores:
        store.wait()


def solution(mesh):
    nx, ny, nz = mesh.shape["gx"], mesh.shape["gy"], mesh.shape["gz"]
    tiles = nx * ny

    def body(
        adjoint_final,
        conductivity,
        step_ratio,
        refine_rate,
        residual,
        sensor_tile,
        sensor_cell,
        substeps,
    ):
        layers, rows, cols = adjoint_final.shape
        steps, listed = residual.shape
        cells = layers * rows
        flat = (cells, cols)
        wide = -(-3 * layers // SUB) * SUB
        narrow = -(-layers // SUB) * SUB
        height = -(-(steps + 2) // SUB) * SUB
        turns = steps - 1
        f32 = jnp.float32
        hbm = pl.BlockSpec(memory_space=pltpu.HBM)
        kept, moved, sens = pl.pallas_call(
            functools.partial(kernel, (nx, ny, nz, layers, rows, cols, steps, listed)),
            out_shape=[jax.ShapeDtypeStruct(flat, f32)] * 3,
            in_specs=[hbm] * 8,
            out_specs=[hbm] * 3,
            scratch_shapes=[
                pltpu.VMEM((6, cells, cols), f32),
                pltpu.VMEM((steps, listed), f32),
                pltpu.VMEM((1, listed), jnp.int32),
                pltpu.VMEM((1, listed), jnp.int32),
                pltpu.SMEM(substeps.shape, jnp.int32),
                pltpu.VMEM((height, cols), f32),
                pltpu.VMEM((tiles, height, cols), f32),
                pltpu.VMEM((2, wide, cols), f32),
                pltpu.VMEM((2, wide, cols), f32),
                pltpu.VMEM((2, SUB, cols), f32),
                pltpu.VMEM((2, SUB, cols), f32),
                pltpu.VMEM((2, 3, rows, cols), f32),
                pltpu.VMEM((turns, cells, cols), f32),
                pltpu.VMEM((turns, 2, narrow, cols), f32),
                pltpu.VMEM((turns, 2, narrow, cols), f32),
                pltpu.VMEM((turns, 2, SUB, cols), f32),
                pltpu.VMEM((turns, 2, SUB, cols), f32),
                pltpu.VMEM((turns, 2, rows, cols), f32),
                pltpu.VMEM((3, cells, cols), f32),
                pltpu.VMEM((2, cells + 2 * SUB, cols), f32),
                pltpu.SemaphoreType.DMA((8,)),
                pltpu.SemaphoreType.DMA((3,)),
                pltpu.SemaphoreType.DMA((tiles,)),
                pltpu.SemaphoreType.DMA((tiles,)),
                pltpu.SemaphoreType.DMA((steps, 6)),
                pltpu.SemaphoreType.DMA((steps, 6)),
            ],
            compiler_params=pltpu.CompilerParams(
                collective_id=0, has_side_effects=True, vmem_limit_bytes=63 * 1024 * 1024
            ),
        )(
            conductivity.reshape(3, *flat),
            adjoint_final.reshape(flat),
            step_ratio.reshape(flat),
            refine_rate.reshape(flat),
            residual,
            sensor_tile.reshape(1, listed),
            sensor_cell.reshape(1, listed),
            substeps,
        )
        shape = adjoint_final.shape
        adjoint = kept.reshape(shape) + moved.reshape(shape)
        return adjoint, sens.reshape(shape) + step_ratio * adjoint

    return jax.shard_map(
        body,
        mesh=mesh,
        in_specs=(
            P("gz", "gx", "gy"),
            P(None, "gz", "gx", "gy"),
            P("gz", "gx", "gy"),
            P("gz", "gx", "gy"),
            P(None, ("gx", "gy")),
            P(("gx", "gy")),
            P(("gx", "gy")),
            P(),
        ),
        out_specs=(P("gz", "gx", "gy"), P("gz", "gx", "gy")),
        check_vma=False,
    )
```

```python
import functools

import jax
import jax.numpy as jnp
from jax import lax
from jax.experimental import pallas as pl
from jax.experimental.pallas import tpu as pltpu
from jax.sharding import PartitionSpec as P

MESH = pl.DeviceIdType.MESH
MOST_TURNS = 6
SUB = 8
NT = (((1,), (1,)), ((), ()))


def harmonic(first, second):
    return 2.0 * first * second / (first + second)


def pieces_of(values):
    high = values.astype(jnp.bfloat16).astype(jnp.float32)
    rest = values - high
    middle = rest.astype(jnp.bfloat16).astype(jnp.float32)
    return high, middle, rest - middle


def kernel(
    sizes,
    cond_hbm,
    adjoint_hbm,
    ratio_hbm,
    rate_hbm,
    res_hbm,
    tile_hbm,
    cell_hbm,
    substeps_hbm,
    kept_out,
    moved_out,
    sens_out,
    base,
    res_in,
    tile_in,
    cell_in,
    substeps_ref,
    sensors,
    gathered,
    first_x,
    first_x_in,
    first_y,
    first_y_in,
    first_z_in,
    send_w,
    send_x,
    recv_x,
    send_y,
    recv_y,
    recv_z,
    results,
    shifted,
    load_sem,
    store_sem,
    sensor_send,
    sensor_recv,
    halo_send,
    halo_recv,
):
    nx, ny, nz, layers, rows, cols, steps, listed = sizes
    cells = layers * rows
    groups_of_rows = cells // SUB
    tiles = nx * ny
    x, y, z = lax.axis_index("gx"), lax.axis_index("gy"), lax.axis_index("gz")
    me = x * ny + y

    loads = [
        pltpu.make_async_copy(src, dst, load_sem.at[k])
        for k, (src, dst) in enumerate(
            (
                (res_hbm, res_in),
                (tile_hbm, tile_in),
                (cell_hbm, cell_in),
                (adjoint_hbm, base.at[3]),
                (ratio_hbm, base.at[4]),
                (cond_hbm, base.at[pl.ds(0, 3)]),
                (rate_hbm, base.at[5]),
                (substeps_hbm, substeps_ref),
            )
        )
    ]
    for load in loads:
        load.start()

    for ref in (first_x_in, first_y_in, first_z_in, recv_x, recv_y, recv_z, sensors, shifted):
        ref[...] = jnp.zeros_like(ref)

    sides = (
        (0, nx, x, -1),
        (0, nx, x, 1),
        (1, ny, y, -1),
        (1, ny, y, 1),
        (2, nz, z, -1),
        (2, nz, z, 1),
    )

    def device_at(axis, step):
        place = [x, y, z]
        place[axis] = place[axis] + step
        return tuple(place)

    def inside(count, place, step):
        return place > 0 if step < 0 else place < count - 1

    barrier = pltpu.get_barrier_semaphore()

    def sensor_peer(offset):
        there = lax.rem(me + offset, tiles)
        return (lax.div(there, ny), lax.rem(there, ny), z)

    for offset in range(1, tiles):
        pl.semaphore_signal(barrier, inc=1, device_id=sensor_peer(offset), device_id_type=MESH)
    for axis, count, place, step in sides[4:]:

        @pl.when(inside(count, place, step))
        def _():
            pl.semaphore_signal(
                barrier, inc=1, device_id=device_at(axis, step), device_id_type=MESH
            )

    for load in loads[:3]:
        load.wait()
    per = max(1, cols // listed)
    lane = lax.broadcasted_iota(jnp.int32, (1, cols), 1)
    cell = cell_in[...]
    grid_layers_rows = nz * cells
    key = tile_in[...] * grid_layers_rows + lax.div(cell, cols)
    column = lax.rem(cell, cols)
    for slot in range(per):
        here = pl.ds(slot * listed, listed)
        sensors[0:steps, here] = res_in[...]
        sensors[steps : steps + 1, here] = key.astype(jnp.float32)
        sensors[steps + 1 : steps + 2, here] = column.astype(jnp.float32)
    if per > 1:
        mine = lax.div(lane, listed) == lax.rem(me, per)
        sensors[...] = jnp.where(mine, sensors[...], 0.0)
    gathered[me] = sensors[...]

    neighbours = (
        (tiles - 1)
        + (z > 0).astype(jnp.int32)
        + (z < nz - 1).astype(jnp.int32)
    )
    pl.semaphore_wait(barrier, neighbours)

    def sensor_copy(offset):
        return pltpu.make_async_remote_copy(
            src_ref=sensors,
            dst_ref=gathered.at[me],
            send_sem=sensor_send.at[offset],
            recv_sem=sensor_recv.at[offset],
            device_id=sensor_peer(offset),
            device_id_type=MESH,
        )

    def sensor_arrival(offset):
        origin = lax.rem(me + (tiles - offset), tiles)
        return pltpu.make_async_remote_copy(
            src_ref=sensors,
            dst_ref=gathered.at[origin],
            send_sem=sensor_send.at[offset],
            recv_sem=sensor_recv.at[offset],
            device_id=sensor_peer(offset),
            device_id_type=MESH,
        )

    for offset in range(1, tiles):
        sensor_copy(offset).start()

    for load in loads[3:]:
        load.wait()
    lanes = lax.broadcasted_iota(jnp.int32, (SUB, cols), 1)

    def pack_columns(arrays):
        to_left = jnp.zeros((SUB, cols), jnp.float32)
        to_right = jnp.zeros((SUB, cols), jnp.float32)
        spot = 0
        for array in arrays:
            for part in range(groups_of_rows):
                block = array[part * SUB : (part + 1) * SUB, :]
                left = pltpu.roll(block, spot % cols, 1)
                right = pltpu.roll(block, (spot + 2) % cols, 1)
                to_left = jnp.where(lanes == spot, left, to_left)
                to_right = jnp.where(lanes == spot + 1, right, to_right)
                spot += 2
        return to_left, to_right

    def unpack_columns(packed, spot):
        return jnp.concatenate(
            [
                pltpu.roll(packed, (cols - 2 * (spot + part) - 1) % cols, 1)
                for part in range(groups_of_rows)
            ],
            axis=0,
        )

    def pick_rows(array, row):
        return jnp.concatenate(
            [array[level * rows + row : level * rows + row + 1, :] for level in range(layers)],
            axis=0,
        )

    def spread_rows(low, high):
        half = rows // 2
        parts = []
        for level in range(layers):
            parts.append(jnp.broadcast_to(low[level : level + 1, :], (half, cols)))
            parts.append(jnp.broadcast_to(high[level : level + 1, :], (rows - half, cols)))
        return jnp.concatenate(parts, axis=0)

    c0, c1, c2 = base[0], base[1], base[2]
    adjoint, ratio, rate = base[3], base[4], base[5]

    def halo_copies(turn):
        copies = []
        for side, (axis, count, place, step) in enumerate(sides):
            way = side % 2
            if turn == 0:
                source, target = (
                    (first_x.at[way], first_x_in.at[1 - way]),
                    (first_y.at[way], first_y_in.at[1 - way]),
                    (
                        base.at[pl.ds(2, 3), pl.ds(way * (cells - rows), rows)],
                        first_z_in.at[1 - way],
                    ),
                )[axis]
            else:
                at = turn - 1
                source, target = (
                    (send_x.at[at, way], recv_x.at[at, 1 - way]),
                    (send_y.at[at, way], recv_y.at[at, 1 - way]),
                    (
                        send_w.at[at, pl.ds(way * (cells - rows), rows)],
                        recv_z.at[at, 1 - way],
                    ),
                )[axis]
            copy = pltpu.make_async_remote_copy(
                src_ref=source,
                dst_ref=target,
                send_sem=halo_send.at[turn, side],
                recv_sem=halo_recv.at[turn, 2 * axis + 1 - way],
                device_id=device_at(axis, step),
                device_id_type=MESH,
            )
            arrival = pltpu.make_async_remote_copy(
                src_ref=source,
                dst_ref=(
                    (first_x_in, first_y_in, first_z_in)[axis].at[way]
                    if turn == 0
                    else (recv_x, recv_y, recv_z)[axis].at[turn - 1, way]
                ),
                send_sem=halo_send.at[turn, side],
                recv_sem=halo_recv.at[turn, side],
                device_id=device_at(axis, step),
                device_id_type=MESH,
            )
            copies.append((inside(count, place, step), copy, arrival))
        return copies

    def start(copies, chosen):
        for side in chosen:
            valid, copy, _ = copies[side]
            pl.when(valid)(copy.start)

    def arrive(copies, chosen):
        for side in chosen:
            valid, _, arrival = copies[side]
            pl.when(valid)(arrival.wait_recv)

    def sent(copies):
        for valid, copy, _ in copies:
            pl.when(valid)(copy.wait_send)

    copies = halo_copies(0)
    start(copies, (4, 5))
    for k, array in enumerate((adjoint, ratio, c0)):
        first_x[0, k * layers : (k + 1) * layers, :] = pick_rows(array, 0)
        first_x[1, k * layers : (k + 1) * layers, :] = pick_rows(array, rows - 1)
    left, right = pack_columns((adjoint, ratio, c1))
    first_y[0] = left
    first_y[1] = right

    start(copies, (2, 3, 0, 1))

    full = (cells, cols)
    row_in = lax.rem(lax.broadcasted_iota(jnp.int32, full, 0), rows)
    col_in = lax.broadcasted_iota(jnp.int32, full, 1)
    top, bottom = row_in == 0, row_in == rows - 1
    first_col, last_col = col_in == 0, col_in == cols - 1

    def next_row(array):
        return pltpu.roll(array, cells - 1, 0)

    def prev_row(array):
        return pltpu.roll(array, 1, 0)

    def next_col(array):
        return pltpu.roll(array, cols - 1, 1)

    def prev_col(array):
        return pltpu.roll(array, 1, 1)

    row_next = jnp.where(bottom, 0.0, harmonic(c0, next_row(c0)))
    row_prev = prev_row(row_next)
    col_next = jnp.where(last_col, 0.0, harmonic(c1, next_col(c1)))
    col_prev = prev_col(col_next)
    between = harmonic(c2[: cells - rows], c2[rows:])
    no_layer = jnp.zeros((rows, cols), jnp.float32)
    rate_next_row = jnp.where(bottom, 0.0, next_row(rate))
    rate_prev_row = jnp.where(top, 0.0, prev_row(rate))
    rate_next_col = jnp.where(last_col, 0.0, next_col(rate))
    rate_prev_col = jnp.where(first_col, 0.0, prev_col(rate))
    around = (
        4.0
        - top.astype(jnp.float32)
        - bottom.astype(jnp.float32)
        - first_col.astype(jnp.float32)
        - last_col.astype(jnp.float32)
    )
    stay = 1.0 - around * rate
    turns = jnp.full(full, substeps_ref[x, y])
    inner_faces = (
        row_next
        + row_prev
        + col_next
        + col_prev
        + jnp.concatenate([between, no_layer], axis=0)
        + jnp.concatenate([no_layer, between], axis=0)
    )

    def halves(field, turn):
        half = turn % 2
        shifted[half, SUB : SUB + cells, :] = field
        below = shifted[half, SUB + 1 : SUB + 1 + cells, :]
        above = shifted[half, SUB - 1 : SUB - 1 + cells, :]
        around_it = (rate_next_row * below + rate_prev_row * above) + (
            rate_next_col * next_col(field) + rate_prev_col * prev_col(field)
        )
        return stay * field, around_it

    def refine(field, count):
        for turn in range(count):
            kept, moved = halves(field, turn)
            field = jnp.where(turns > turn, kept + moved, field)
        return field

    def inner(field, weighted, own):
        return (
            own * field
            + (row_next * next_row(weighted) + row_prev * prev_row(weighted))
            + (col_next * next_col(weighted) + col_prev * prev_col(weighted))
            + jnp.concatenate([between * weighted[rows:], no_layer], axis=0)
            + jnp.concatenate([no_layer, between * weighted[: cells - rows]], axis=0)
        )

    row_key = (me * grid_layers_rows + z * cells).astype(jnp.float32)

    def keys(count, start_at):
        place = lax.broadcasted_iota(jnp.int32, (count, cols), 0).astype(jnp.float32)
        return place + (row_key + start_at)

    for offset in range(1, tiles):
        sensor_arrival(offset).wait_recv()
    blocks = []
    folded = max(1, tiles // per)
    for block in range(folded):
        total = gathered[block * per]
        for slot in range(1, per):
            total = total + gathered[block * per + slot]
        blocks.append(total)
    key_rows = [total[steps : steps + 1, :] for total in blocks]
    col_rows = [total[steps + 1 : steps + 2, :] for total in blocks]
    split = [pieces_of(total[0:steps, :]) for total in blocks]
    col_ids = lax.broadcasted_iota(jnp.int32, (cols, cols), 0).astype(jnp.float32)
    in_column = jnp.concatenate(
        [jnp.where(col_ids == line, 1.0, 0.0).astype(jnp.bfloat16) for line in col_rows], axis=1
    )

    def placed(row_keys, sensor_keys, step, piece):
        return jnp.concatenate(
            [
                jnp.where(
                    row_keys == line, parts[piece][step : step + 1, :], 0.0
                ).astype(jnp.bfloat16)
                for line, parts in zip(sensor_keys, split)
            ],
            axis=1,
        )

    def source_of(row_keys, sensor_keys, columns, step):
        total = None
        for piece in range(3):
            part = lax.dot_general(
                placed(row_keys, sensor_keys, step, piece),
                columns,
                NT,
                preferred_element_type=jnp.float32,
            )
            total = part if total is None else total + part
        return total

    last = steps - 1
    own_keys = keys(cells, 0.0)
    level_of = lax.broadcasted_iota(jnp.int32, (2 * layers, cols), 0)
    beside = (ny * grid_layers_rows)
    side_keys = row_key + jnp.where(
        level_of < layers,
        level_of * rows + (rows - 1 - beside),
        (level_of - layers) * rows + beside,
    ).astype(jnp.float32)
    wide_keys = jnp.concatenate(
        [
            own_keys,
            keys(rows, -float(rows)),
            keys(rows, float(cells)),
            side_keys,
            jnp.full((2 * layers, cols), -1.0, jnp.float32),
        ],
        axis=0,
    )
    wide = source_of(wide_keys, key_rows, in_column, last)
    far = float(tiles * grid_layers_rows * 4)
    moved_keys = [
        jnp.where(
            col_line == cols - 1.0,
            key_line + float(grid_layers_rows),
            jnp.where(col_line == 0.0, key_line - float(grid_layers_rows), -far),
        )
        for key_line, col_line in zip(key_rows, col_rows)
    ]
    at_edges = jnp.concatenate(
        [
            jnp.where(col_ids == (cols - 1.0) - line, 1.0, 0.0).astype(jnp.bfloat16)
            for line in col_rows
        ],
        axis=1,
    )
    edge = source_of(own_keys, moved_keys, at_edges, last)

    arrive(copies, (0, 1, 4, 5))
    row_halo = spread_rows(
        first_x_in[0, 2 * layers : 3 * layers, :], first_x_in[1, 2 * layers : 3 * layers, :]
    )
    row_face = jnp.where(jnp.logical_or(top, bottom), harmonic(c0, row_halo), 0.0)
    low_face = harmonic(c2[:rows], first_z_in[0, 0])
    high_face = harmonic(c2[cells - rows :], first_z_in[1, 0])
    middle = cells - 2 * rows

    def with_ends(low, high):
        parts = [low]
        if middle > 0:
            parts.append(jnp.zeros((middle, cols), jnp.float32))
        return jnp.concatenate(parts + [high], axis=0)

    near_faces = inner_faces + row_face + with_ends(low_face, high_face)
    row_values = spread_rows(
        first_x_in[0, layers : 2 * layers, :]
        * (first_x_in[0, 0:layers, :] + wide[cells + 2 * rows : cells + 2 * rows + layers]),
        first_x_in[1, layers : 2 * layers, :]
        * (
            first_x_in[1, 0:layers, :]
            + wide[cells + 2 * rows + layers : cells + 2 * rows + 2 * layers]
        ),
    )
    low_values = first_z_in[0, 2] * (first_z_in[0, 1] + wide[cells : cells + rows])
    high_values = first_z_in[1, 2] * (first_z_in[1, 1] + wide[cells + rows : cells + 2 * rows])

    def outer(row_values, low_values, high_values):
        return row_face * row_values + with_ends(
            low_face * low_values, high_face * high_values
        )

    arrive(copies, (2, 3))
    packed = first_y_in[0] + first_y_in[1]
    col_halo = unpack_columns(packed, 2 * groups_of_rows)
    col_face = jnp.where(jnp.logical_or(first_col, last_col), harmonic(c1, col_halo), 0.0)
    own = 1.0 - ratio * (near_faces + col_face)

    field = adjoint + wide[:cells]
    cols_adjoint = unpack_columns(packed, 0)
    cols_ratio = unpack_columns(packed, groups_of_rows)
    field = (
        inner(field, ratio * field, own)
        + outer(row_values, low_values, high_values)
        + col_face * (cols_ratio * (cols_adjoint + edge))
    )
    next_source = source_of(own_keys, key_rows, in_column, last - 1)
    field = refine(field, MOST_TURNS)
    sens = ratio * field

    stores = [
        pltpu.make_async_copy(results.at[k], out, store_sem.at[k])
        for k, out in enumerate((kept_out, moved_out, sens_out))
    ]
    pending = [copies]
    sources = {last - 1: next_source}
    for turn in range(1, steps):
        step = last - turn
        field = field + sources[step]
        weighted = ratio * field
        copies = halo_copies(turn)
        at = turn - 1
        left, right = pack_columns((weighted,))
        send_y[at, 0] = left
        send_y[at, 1] = right
        start(copies, (2, 3))
        send_w[at] = weighted
        start(copies, (4, 5))
        send_x[at, 0, 0:layers, :] = pick_rows(weighted, 0)
        send_x[at, 1, 0:layers, :] = pick_rows(weighted, rows - 1)
        start(copies, (0, 1))
        pending.append(copies)
        if step == 0:
            results[2] = sens
            stores[2].start()
        field = inner(field, weighted, own)
        if step > 0:
            sources[step - 1] = source_of(own_keys, key_rows, in_column, step - 1)
        arrive(copies, (0, 1, 4, 5))
        field = field + outer(
            spread_rows(recv_x[at, 0, 0:layers, :], recv_x[at, 1, 0:layers, :]),
            recv_z[at, 0],
            recv_z[at, 1],
        )
        arrive(copies, (2, 3))
        field = field + col_face * unpack_columns(recv_y[at, 0] + recv_y[at, 1], 0)
        if step > 0:
            field = refine(field, MOST_TURNS)
            sens = sens + ratio * field

    field = refine(field, MOST_TURNS - 1)
    kept, moved = halves(field, MOST_TURNS - 1)
    active = turns > MOST_TURNS - 1
    results[0] = jnp.where(active, kept, field)
    results[1] = jnp.where(active, moved, 0.0)
    for store in stores[:2]:
        store.start()
    for offset in range(1, tiles):
        sensor_copy(offset).wait_send()
    for copies in pending:
        sent(copies)
    for store in stores:
        store.wait()


def solution(mesh):
    nx, ny, nz = mesh.shape["gx"], mesh.shape["gy"], mesh.shape["gz"]
    tiles = nx * ny

    def body(
        adjoint_final,
        conductivity,
        step_ratio,
        refine_rate,
        residual,
        sensor_tile,
        sensor_cell,
        substeps,
    ):
        layers, rows, cols = adjoint_final.shape
        steps, listed = residual.shape
        cells = layers * rows
        flat = (cells, cols)
        wide = -(-3 * layers // SUB) * SUB
        narrow = -(-layers // SUB) * SUB
        height = -(-(steps + 2) // SUB) * SUB
        turns = steps - 1
        f32 = jnp.float32
        hbm = pl.BlockSpec(memory_space=pltpu.HBM)
        kept, moved, sens = pl.pallas_call(
            functools.partial(kernel, (nx, ny, nz, layers, rows, cols, steps, listed)),
            out_shape=[jax.ShapeDtypeStruct(flat, f32)] * 3,
            in_specs=[hbm] * 8,
            out_specs=[hbm] * 3,
            scratch_shapes=[
                pltpu.VMEM((6, cells, cols), f32),
                pltpu.VMEM((steps, listed), f32),
                pltpu.VMEM((1, listed), jnp.int32),
                pltpu.VMEM((1, listed), jnp.int32),
                pltpu.SMEM(substeps.shape, jnp.int32),
                pltpu.VMEM((height, cols), f32),
                pltpu.VMEM((tiles, height, cols), f32),
                pltpu.VMEM((2, wide, cols), f32),
                pltpu.VMEM((2, wide, cols), f32),
                pltpu.VMEM((2, SUB, cols), f32),
                pltpu.VMEM((2, SUB, cols), f32),
                pltpu.VMEM((2, 3, rows, cols), f32),
                pltpu.VMEM((turns, cells, cols), f32),
                pltpu.VMEM((turns, 2, narrow, cols), f32),
                pltpu.VMEM((turns, 2, narrow, cols), f32),
                pltpu.VMEM((turns, 2, SUB, cols), f32),
                pltpu.VMEM((turns, 2, SUB, cols), f32),
                pltpu.VMEM((turns, 2, rows, cols), f32),
                pltpu.VMEM((3, cells, cols), f32),
                pltpu.VMEM((2, cells + 2 * SUB, cols), f32),
                pltpu.SemaphoreType.DMA((8,)),
                pltpu.SemaphoreType.DMA((3,)),
                pltpu.SemaphoreType.DMA((tiles,)),
                pltpu.SemaphoreType.DMA((tiles,)),
                pltpu.SemaphoreType.DMA((steps, 6)),
                pltpu.SemaphoreType.DMA((steps, 6)),
            ],
            compiler_params=pltpu.CompilerParams(
                collective_id=0, has_side_effects=True, vmem_limit_bytes=63 * 1024 * 1024
            ),
        )(
            conductivity.reshape(3, *flat),
            adjoint_final.reshape(flat),
            step_ratio.reshape(flat),
            refine_rate.reshape(flat),
            residual,
            sensor_tile.reshape(1, listed),
            sensor_cell.reshape(1, listed),
            substeps,
        )
        shape = adjoint_final.shape
        adjoint = kept + moved
        sensitivity = sens + step_ratio.reshape(flat) * adjoint
        return adjoint.reshape(shape), sensitivity.reshape(shape)

    return jax.shard_map(
        body,
        mesh=mesh,
        in_specs=(
            P("gz", "gx", "gy"),
            P(None, "gz", "gx", "gy"),
            P("gz", "gx", "gy"),
            P("gz", "gx", "gy"),
            P(None, ("gx", "gy")),
            P(("gx", "gy")),
            P(("gx", "gy")),
            P(),
        ),
        out_specs=(P("gz", "gx", "gy"), P("gz", "gx", "gy")),
        check_vma=False,
    )
```

```python
import functools

import jax
import jax.numpy as jnp
from jax import lax
from jax.experimental import pallas as pl
from jax.experimental.pallas import tpu as pltpu
from jax.sharding import PartitionSpec as P

MESH = pl.DeviceIdType.MESH
MOST_TURNS = 6
SUB = 8
NT = (((1,), (1,)), ((), ()))


def harmonic(first, second):
    return 2.0 * first * second / (first + second)


def pieces_of(values):
    high = values.astype(jnp.bfloat16).astype(jnp.float32)
    rest = values - high
    middle = rest.astype(jnp.bfloat16).astype(jnp.float32)
    return high, middle, rest - middle


def kernel(
    sizes,
    cond_hbm,
    adjoint_hbm,
    ratio_hbm,
    rate_hbm,
    res_hbm,
    tile_hbm,
    cell_hbm,
    substeps_hbm,
    kept_out,
    moved_out,
    sens_out,
    base,
    res_in,
    tile_in,
    cell_in,
    substeps_ref,
    sensors,
    gathered,
    first_x,
    first_x_in,
    first_y,
    first_y_in,
    first_z_in,
    send_w,
    send_x,
    recv_x,
    send_y,
    recv_y,
    recv_z,
    results,
    load_sem,
    store_sem,
    sensor_send,
    sensor_recv,
    halo_send,
    halo_recv,
):
    nx, ny, nz, layers, rows, cols, steps, listed = sizes
    cells = layers * rows
    groups_of_rows = cells // SUB
    tiles = nx * ny
    x, y, z = lax.axis_index("gx"), lax.axis_index("gy"), lax.axis_index("gz")
    me = x * ny + y

    loads = [
        pltpu.make_async_copy(src, dst, load_sem.at[k])
        for k, (src, dst) in enumerate(
            (
                (res_hbm, res_in),
                (tile_hbm, tile_in),
                (cell_hbm, cell_in),
                (adjoint_hbm, base.at[3]),
                (ratio_hbm, base.at[4]),
                (cond_hbm, base.at[pl.ds(0, 3)]),
                (rate_hbm, base.at[5]),
                (substeps_hbm, substeps_ref),
            )
        )
    ]
    for ref in (first_x_in, first_y_in, first_z_in, recv_x, recv_y, recv_z, sensors):
        ref[...] = jnp.zeros_like(ref)

    sides = (
        (0, nx, x, -1),
        (0, nx, x, 1),
        (1, ny, y, -1),
        (1, ny, y, 1),
        (2, nz, z, -1),
        (2, nz, z, 1),
    )

    def device_at(axis, step):
        place = [x, y, z]
        place[axis] = place[axis] + step
        return tuple(place)

    def inside(count, place, step):
        return place > 0 if step < 0 else place < count - 1

    barrier = pltpu.get_barrier_semaphore()

    def sensor_peer(offset):
        there = lax.rem(me + offset, tiles)
        return (lax.div(there, ny), lax.rem(there, ny), z)

    for offset in range(1, tiles):
        pl.semaphore_signal(barrier, inc=1, device_id=sensor_peer(offset), device_id_type=MESH)
    for axis, count, place, step in sides[4:]:

        @pl.when(inside(count, place, step))
        def _():
            pl.semaphore_signal(
                barrier, inc=1, device_id=device_at(axis, step), device_id_type=MESH
            )

    for load in loads:
        load.start()

    for load in loads[:3]:
        load.wait()
    per = max(1, cols // listed)
    lane = lax.broadcasted_iota(jnp.int32, (1, cols), 1)
    cell = cell_in[...]
    grid_layers_rows = nz * cells
    key = tile_in[...] * grid_layers_rows + lax.div(cell, cols)
    column = lax.rem(cell, cols)
    for slot in range(per):
        here = pl.ds(slot * listed, listed)
        sensors[0:steps, here] = res_in[...]
        sensors[steps : steps + 1, here] = key.astype(jnp.float32)
        sensors[steps + 1 : steps + 2, here] = column.astype(jnp.float32)
    if per > 1:
        mine = lax.div(lane, listed) == lax.rem(me, per)
        sensors[...] = jnp.where(mine, sensors[...], 0.0)
    gathered[me] = sensors[...]

    neighbours = (
        (tiles - 1)
        + (z > 0).astype(jnp.int32)
        + (z < nz - 1).astype(jnp.int32)
    )
    pl.semaphore_wait(barrier, neighbours)

    def sensor_copy(offset):
        return pltpu.make_async_remote_copy(
            src_ref=sensors,
            dst_ref=gathered.at[me],
            send_sem=sensor_send.at[offset],
            recv_sem=sensor_recv.at[offset],
            device_id=sensor_peer(offset),
            device_id_type=MESH,
        )

    def sensor_arrival(offset):
        origin = lax.rem(me + (tiles - offset), tiles)
        return pltpu.make_async_remote_copy(
            src_ref=sensors,
            dst_ref=gathered.at[origin],
            send_sem=sensor_send.at[offset],
            recv_sem=sensor_recv.at[offset],
            device_id=sensor_peer(offset),
            device_id_type=MESH,
        )

    for offset in range(1, tiles):
        sensor_copy(offset).start()

    for load in loads[3:]:
        load.wait()
    lanes = lax.broadcasted_iota(jnp.int32, (SUB, cols), 1)

    def pack_columns(arrays):
        to_left = jnp.zeros((SUB, cols), jnp.float32)
        to_right = jnp.zeros((SUB, cols), jnp.float32)
        spot = 0
        for array in arrays:
            for part in range(groups_of_rows):
                block = array[part * SUB : (part + 1) * SUB, :]
                left = pltpu.roll(block, spot % cols, 1)
                right = pltpu.roll(block, (spot + 2) % cols, 1)
                to_left = jnp.where(lanes == spot, left, to_left)
                to_right = jnp.where(lanes == spot + 1, right, to_right)
                spot += 2
        return to_left, to_right

    def unpack_columns(packed, spot):
        return jnp.concatenate(
            [
                pltpu.roll(packed, (cols - 2 * (spot + part) - 1) % cols, 1)
                for part in range(groups_of_rows)
            ],
            axis=0,
        )

    def pick_rows(array, row):
        return jnp.concatenate(
            [array[level * rows + row : level * rows + row + 1, :] for level in range(layers)],
            axis=0,
        )

    def spread_rows(low, high):
        half = rows // 2
        parts = []
        for level in range(layers):
            parts.append(jnp.broadcast_to(low[level : level + 1, :], (half, cols)))
            parts.append(jnp.broadcast_to(high[level : level + 1, :], (rows - half, cols)))
        return jnp.concatenate(parts, axis=0)

    c0, c1, c2 = base[0], base[1], base[2]
    adjoint, ratio, rate = base[3], base[4], base[5]

    def halo_copies(turn):
        copies = []
        for side, (axis, count, place, step) in enumerate(sides):
            way = side % 2
            if turn == 0:
                source, target = (
                    (first_x.at[way], first_x_in.at[1 - way]),
                    (first_y.at[way], first_y_in.at[1 - way]),
                    (
                        base.at[pl.ds(2, 3), pl.ds(way * (cells - rows), rows)],
                        first_z_in.at[1 - way],
                    ),
                )[axis]
            else:
                at = turn - 1
                source, target = (
                    (send_x.at[at, way], recv_x.at[at, 1 - way]),
                    (send_y.at[at, way], recv_y.at[at, 1 - way]),
                    (
                        send_w.at[at, pl.ds(way * (cells - rows), rows)],
                        recv_z.at[at, 1 - way],
                    ),
                )[axis]
            copy = pltpu.make_async_remote_copy(
                src_ref=source,
                dst_ref=target,
                send_sem=halo_send.at[turn, side],
                recv_sem=halo_recv.at[turn, 2 * axis + 1 - way],
                device_id=device_at(axis, step),
                device_id_type=MESH,
            )
            arrival = pltpu.make_async_remote_copy(
                src_ref=source,
                dst_ref=(
                    (first_x_in, first_y_in, first_z_in)[axis].at[way]
                    if turn == 0
                    else (recv_x, recv_y, recv_z)[axis].at[turn - 1, way]
                ),
                send_sem=halo_send.at[turn, side],
                recv_sem=halo_recv.at[turn, side],
                device_id=device_at(axis, step),
                device_id_type=MESH,
            )
            copies.append((inside(count, place, step), copy, arrival))
        return copies

    def start(copies, chosen):
        for side in chosen:
            valid, copy, _ = copies[side]
            pl.when(valid)(copy.start)

    def arrive(copies):
        for valid, _, arrival in copies:
            pl.when(valid)(arrival.wait_recv)

    def sent(copies):
        for valid, copy, _ in copies:
            pl.when(valid)(copy.wait_send)

    copies = halo_copies(0)
    start(copies, (4, 5))
    left, right = pack_columns((adjoint, ratio, c1))
    first_y[0] = left
    first_y[1] = right

    start(copies, (2, 3))
    for k, array in enumerate((adjoint, ratio, c0)):
        first_x[0, k * layers : (k + 1) * layers, :] = pick_rows(array, 0)
        first_x[1, k * layers : (k + 1) * layers, :] = pick_rows(array, rows - 1)
    start(copies, (0, 1))

    full = (cells, cols)
    row_in = lax.rem(lax.broadcasted_iota(jnp.int32, full, 0), rows)
    col_in = lax.broadcasted_iota(jnp.int32, full, 1)
    top, bottom = row_in == 0, row_in == rows - 1
    first_col, last_col = col_in == 0, col_in == cols - 1

    def next_row(array):
        return pltpu.roll(array, cells - 1, 0)

    def prev_row(array):
        return pltpu.roll(array, 1, 0)

    def next_col(array):
        return pltpu.roll(array, cols - 1, 1)

    def prev_col(array):
        return pltpu.roll(array, 1, 1)

    row_next = jnp.where(bottom, 0.0, harmonic(c0, next_row(c0)))
    row_prev = prev_row(row_next)
    col_next = jnp.where(last_col, 0.0, harmonic(c1, next_col(c1)))
    col_prev = prev_col(col_next)
    between = harmonic(c2[: cells - rows], c2[rows:])
    no_layer = jnp.zeros((rows, cols), jnp.float32)
    rate_next_row = jnp.where(bottom, 0.0, next_row(rate))
    rate_prev_row = jnp.where(top, 0.0, prev_row(rate))
    rate_next_col = jnp.where(last_col, 0.0, next_col(rate))
    rate_prev_col = jnp.where(first_col, 0.0, prev_col(rate))
    around = (
        4.0
        - top.astype(jnp.float32)
        - bottom.astype(jnp.float32)
        - first_col.astype(jnp.float32)
        - last_col.astype(jnp.float32)
    )
    stay = 1.0 - around * rate
    turns = jnp.full(full, substeps_ref[x, y])
    inner_faces = (
        row_next
        + row_prev
        + col_next
        + col_prev
        + jnp.concatenate([between, no_layer], axis=0)
        + jnp.concatenate([no_layer, between], axis=0)
    )

    def halves(field):
        around_it = (rate_next_row * next_row(field) + rate_prev_row * prev_row(field)) + (
            rate_next_col * next_col(field) + rate_prev_col * prev_col(field)
        )
        return stay * field, around_it

    def refine(field, count):
        for turn in range(count):
            kept, moved = halves(field)
            field = jnp.where(turns > turn, kept + moved, field)
        return field

    def inner(field, weighted, own):
        return (
            own * field
            + (row_next * next_row(weighted) + row_prev * prev_row(weighted))
            + (col_next * next_col(weighted) + col_prev * prev_col(weighted))
            + jnp.concatenate([between * weighted[rows:], no_layer], axis=0)
            + jnp.concatenate([no_layer, between * weighted[: cells - rows]], axis=0)
        )

    row_key = (me * grid_layers_rows + z * cells).astype(jnp.float32)

    def keys(count, start_at):
        place = lax.broadcasted_iota(jnp.int32, (count, cols), 0).astype(jnp.float32)
        return place + (row_key + start_at)

    for offset in range(1, tiles):
        sensor_arrival(offset).wait_recv()
    blocks = []
    folded = max(1, tiles // per)
    for block in range(folded):
        total = gathered[block * per]
        for slot in range(1, per):
            total = total + gathered[block * per + slot]
        blocks.append(total)
    key_rows = [total[steps : steps + 1, :] for total in blocks]
    col_rows = [total[steps + 1 : steps + 2, :] for total in blocks]
    split = [pieces_of(total[0:steps, :]) for total in blocks]
    col_ids = lax.broadcasted_iota(jnp.int32, (cols, cols), 0).astype(jnp.float32)
    in_column = jnp.concatenate(
        [jnp.where(col_ids == line, 1.0, 0.0).astype(jnp.bfloat16) for line in col_rows], axis=1
    )

    def placed(row_keys, sensor_keys, step, piece):
        return jnp.concatenate(
            [
                jnp.where(
                    row_keys == line, parts[piece][step : step + 1, :], 0.0
                ).astype(jnp.bfloat16)
                for line, parts in zip(sensor_keys, split)
            ],
            axis=1,
        )

    def source_of(row_keys, sensor_keys, columns, step):
        total = None
        for piece in range(3):
            part = lax.dot_general(
                placed(row_keys, sensor_keys, step, piece),
                columns,
                NT,
                preferred_element_type=jnp.float32,
            )
            total = part if total is None else total + part
        return total

    last = steps - 1
    own_keys = keys(cells, 0.0)
    level_of = lax.broadcasted_iota(jnp.int32, (2 * layers, cols), 0)
    beside = (ny * grid_layers_rows)
    side_keys = row_key + jnp.where(
        level_of < layers,
        level_of * rows + (rows - 1 - beside),
        (level_of - layers) * rows + beside,
    ).astype(jnp.float32)
    wide_keys = jnp.concatenate(
        [
            own_keys,
            keys(rows, -float(rows)),
            keys(rows, float(cells)),
            side_keys,
            jnp.full((2 * layers, cols), -1.0, jnp.float32),
        ],
        axis=0,
    )
    wide = source_of(wide_keys, key_rows, in_column, last)
    far = float(tiles * grid_layers_rows * 4)
    moved_keys = [
        jnp.where(
            col_line == cols - 1.0,
            key_line + float(grid_layers_rows),
            jnp.where(col_line == 0.0, key_line - float(grid_layers_rows), -far),
        )
        for key_line, col_line in zip(key_rows, col_rows)
    ]
    at_edges = jnp.concatenate(
        [
            jnp.where(col_ids == (cols - 1.0) - line, 1.0, 0.0).astype(jnp.bfloat16)
            for line in col_rows
        ],
        axis=1,
    )
    edge = source_of(own_keys, moved_keys, at_edges, last)

    arrive(copies)

    row_halo = spread_rows(
        first_x_in[0, 2 * layers : 3 * layers, :], first_x_in[1, 2 * layers : 3 * layers, :]
    )
    row_face = jnp.where(jnp.logical_or(top, bottom), harmonic(c0, row_halo), 0.0)
    packed = first_y_in[0] + first_y_in[1]
    col_halo = unpack_columns(packed, 2 * groups_of_rows)
    col_face = jnp.where(jnp.logical_or(first_col, last_col), harmonic(c1, col_halo), 0.0)
    low_face = harmonic(c2[:rows], first_z_in[0, 0])
    high_face = harmonic(c2[cells - rows :], first_z_in[1, 0])
    middle = cells - 2 * rows

    def with_ends(low, high):
        parts = [low]
        if middle > 0:
            parts.append(jnp.zeros((middle, cols), jnp.float32))
        return jnp.concatenate(parts + [high], axis=0)

    all_faces = inner_faces + row_face + col_face + with_ends(low_face, high_face)
    own = 1.0 - ratio * all_faces

    def outer(row_values, col_values, low_values, high_values):
        return (
            row_face * row_values
            + col_face * col_values
            + with_ends(low_face * low_values, high_face * high_values)
        )

    field = adjoint + wide[:cells]
    low_src = wide[cells : cells + rows]
    high_src = wide[cells + rows : cells + 2 * rows]
    side_src = wide[cells + 2 * rows : cells + 2 * rows + 2 * layers]
    rows_low = first_x_in[0, layers : 2 * layers, :] * (
        first_x_in[0, 0:layers, :] + side_src[:layers]
    )
    rows_high = first_x_in[1, layers : 2 * layers, :] * (
        first_x_in[1, 0:layers, :] + side_src[layers:]
    )
    cols_adjoint = unpack_columns(packed, 0)
    cols_ratio = unpack_columns(packed, groups_of_rows)
    field = inner(field, ratio * field, own) + outer(
        spread_rows(rows_low, rows_high),
        cols_ratio * (cols_adjoint + edge),
        first_z_in[0, 2] * (first_z_in[0, 1] + low_src),
        first_z_in[1, 2] * (first_z_in[1, 1] + high_src),
    )
    next_source = source_of(own_keys, key_rows, in_column, last - 1)
    field = refine(field, MOST_TURNS)
    sens = ratio * field

    pending = [copies]
    sources = {last - 1: next_source}
    for turn in range(1, steps):
        step = last - turn
        field = field + sources[step]
        weighted = ratio * field
        copies = halo_copies(turn)
        at = turn - 1
        send_w[at] = weighted
        start(copies, (4, 5))
        left, right = pack_columns((weighted,))
        send_y[at, 0] = left
        send_y[at, 1] = right
        start(copies, (2, 3))
        send_x[at, 0, 0:layers, :] = pick_rows(weighted, 0)
        send_x[at, 1, 0:layers, :] = pick_rows(weighted, rows - 1)
        start(copies, (0, 1))
        pending.append(copies)
        field = inner(field, weighted, own)
        if step > 0:
            sources[step - 1] = source_of(own_keys, key_rows, in_column, step - 1)
        arrive(copies)
        field = field + outer(
            spread_rows(recv_x[at, 0, 0:layers, :], recv_x[at, 1, 0:layers, :]),
            unpack_columns(recv_y[at, 0] + recv_y[at, 1], 0),
            recv_z[at, 0],
            recv_z[at, 1],
        )
        if step > 0:
            field = refine(field, MOST_TURNS)
            sens = sens + ratio * field

    field = refine(field, MOST_TURNS - 1)
    kept, moved = halves(field)
    active = turns > MOST_TURNS - 1
    results[0] = jnp.where(active, kept, field)
    results[1] = jnp.where(active, moved, 0.0)
    results[2] = sens
    stores = [
        pltpu.make_async_copy(results.at[k], out, store_sem.at[k])
        for k, out in enumerate((kept_out, moved_out, sens_out))
    ]
    for store in stores:
        store.start()
    for offset in range(1, tiles):
        sensor_copy(offset).wait_send()
    for copies in pending:
        sent(copies)
    for store in stores:
        store.wait()


def solution(mesh):
    nx, ny, nz = mesh.shape["gx"], mesh.shape["gy"], mesh.shape["gz"]
    tiles = nx * ny

    def body(
        adjoint_final,
        conductivity,
        step_ratio,
        refine_rate,
        residual,
        sensor_tile,
        sensor_cell,
        substeps,
    ):
        layers, rows, cols = adjoint_final.shape
        steps, listed = residual.shape
        cells = layers * rows
        flat = (cells, cols)
        wide = -(-3 * layers // SUB) * SUB
        narrow = -(-layers // SUB) * SUB
        height = -(-(steps + 2) // SUB) * SUB
        turns = steps - 1
        f32 = jnp.float32
        hbm = pl.BlockSpec(memory_space=pltpu.HBM)
        kept, moved, sens = pl.pallas_call(
            functools.partial(kernel, (nx, ny, nz, layers, rows, cols, steps, listed)),
            out_shape=[jax.ShapeDtypeStruct(flat, f32)] * 3,
            in_specs=[hbm] * 8,
            out_specs=[hbm] * 3,
            scratch_shapes=[
                pltpu.VMEM((6, cells, cols), f32),
                pltpu.VMEM((steps, listed), f32),
                pltpu.VMEM((1, listed), jnp.int32),
                pltpu.VMEM((1, listed), jnp.int32),
                pltpu.SMEM(substeps.shape, jnp.int32),
                pltpu.VMEM((height, cols), f32),
                pltpu.VMEM((tiles, height, cols), f32),
                pltpu.VMEM((2, wide, cols), f32),
                pltpu.VMEM((2, wide, cols), f32),
                pltpu.VMEM((2, SUB, cols), f32),
                pltpu.VMEM((2, SUB, cols), f32),
                pltpu.VMEM((2, 3, rows, cols), f32),
                pltpu.VMEM((turns, cells, cols), f32),
                pltpu.VMEM((turns, 2, narrow, cols), f32),
                pltpu.VMEM((turns, 2, narrow, cols), f32),
                pltpu.VMEM((turns, 2, SUB, cols), f32),
                pltpu.VMEM((turns, 2, SUB, cols), f32),
                pltpu.VMEM((turns, 2, rows, cols), f32),
                pltpu.VMEM((3, cells, cols), f32),
                pltpu.SemaphoreType.DMA((8,)),
                pltpu.SemaphoreType.DMA((3,)),
                pltpu.SemaphoreType.DMA((tiles,)),
                pltpu.SemaphoreType.DMA((tiles,)),
                pltpu.SemaphoreType.DMA((steps, 6)),
                pltpu.SemaphoreType.DMA((steps, 6)),
            ],
            compiler_params=pltpu.CompilerParams(
                collective_id=0, has_side_effects=True, vmem_limit_bytes=63 * 1024 * 1024
            ),
        )(
            conductivity.reshape(3, *flat),
            adjoint_final.reshape(flat),
            step_ratio.reshape(flat),
            refine_rate.reshape(flat),
            residual,
            sensor_tile.reshape(1, listed),
            sensor_cell.reshape(1, listed),
            substeps,
        )
        shape = adjoint_final.shape
        adjoint = kept.reshape(shape) + moved.reshape(shape)
        return adjoint, sens.reshape(shape) + step_ratio * adjoint

    return jax.shard_map(
        body,
        mesh=mesh,
        in_specs=(
            P("gz", "gx", "gy"),
            P(None, "gz", "gx", "gy"),
            P("gz", "gx", "gy"),
            P("gz", "gx", "gy"),
            P(None, ("gx", "gy")),
            P(("gx", "gy")),
            P(("gx", "gy")),
            P(),
        ),
        out_specs=(P("gz", "gx", "gy"), P("gz", "gx", "gy")),
        check_vma=False,
    )
```
